256 devices in a mesh: axial: 16 (over z, core), radial: 16 (over y, x).
Axes of the slice: x: 4, y: 4, z: 8, core: 2. Of those that a mesh axis runs over, the one named last changes fastest.
Arguments:
- source: float32 [768, 768, 256], P('axial', 'radial'), may hold values from -6 to 6
- pressure_old: float32 [768, 768, 256], P('axial', 'radial'), may hold values from -6 to 6
- density: float32 [768, 768, 256], P('axial', 'radial'), may hold values from 1 to 50
- radial_forward: float32 [768, 768], P('radial'), may hold values from -13 to 13
- radial_back: float32 [768, 768], P('radial'), may hold values from -13 to 13
- radial_eig: float32 [768], replicated, may hold values from 1e-06 to 4
Outputs:
- pressure: float32 [768, 768, 256], P('axial', 'radial')
The draws below stay inside these ranges and needn't reach their ends.
All inputs are finite; a program needn't handle non-finite values.
Results may differ from the reference program's by a relative error of at most 0.00012.
Values sent between devices are 32-bit elements; how exact they have to be, the bound alone decides.
A program may use at most 128 MiB of HBM per device.

```python
import math
import jax
import jax.numpy as jnp
from jax import lax

NR = 768
NT = 256
NZ = 768


def eigen_values(key, lift_power):
    value_key = jax.random.fold_in(key, 5)
    uniform_draw = jax.random.uniform(value_key, (NR,), jnp.float32)
    position = (uniform_draw - jnp.min(uniform_draw)) / (jnp.max(uniform_draw) - jnp.min(uniform_draw))
    exponent = -6.0 + 6.60206 * position ** lift_power
    return jnp.clip(10.0 ** exponent, 1e-06, 4.0)


def eigen_matrix(key, spread):
    key_diag, key_off, key_scale = jax.random.split(key, 3)
    diagonal = jax.random.uniform(key_diag, (NR,), jnp.float32, 0.8, 1.2)
    offdiag = jax.random.truncated_normal(key_off, -4.0, 4.0, (NR, NR), jnp.float32) * (0.6 / math.sqrt(NR))
    scales = 10.0 ** (spread * jax.random.uniform(key_scale, (NR, 1), jnp.float32))
    return (jnp.diag(diagonal) + offdiag) * scales


def draw_radial_eig(key, part):
    lift_power = 1.0
    return eigen_values(key, lift_power)


def draw_radial_forward(key, part):
    lift_power = 1.0
    spread = 0.0
    values = eigen_values(key, lift_power)
    key = jax.random.fold_in(key, 11)
    matrix = eigen_matrix(key, spread)
    row_weight = jnp.minimum(1.0, 30.0 * values + 0.0006)
    return matrix * row_weight[:, None]


def draw_radial_back(key, part):
    key = jax.random.fold_in(key, 23)
    spread = 0.0
    return eigen_matrix(key, spread)


def shard_levels(rng, extent, cuts, least, largest):
    def one(axis_at, shards_of):
        draws = jax.random.uniform(jax.random.fold_in(jax.random.fold_in(rng, 6), axis_at), (shards_of,), jnp.float32, least / len(cuts), largest / len(cuts))
        return jnp.repeat(jnp.exp(draws), extent[axis_at] // shards_of).reshape((-1,) + (1,) * (len(extent) - axis_at - 1))

    factor_of = one(*cuts[0])
    for cut in cuts[1:]:
        factor_of = factor_of * one(*cut)
    return factor_of


def bell_draw(rng, extent, width, reach, cuts=(), held_as=jnp.bfloat16):
    array = width * jax.random.normal(rng, extent, jnp.float32)
    if cuts:
        array = array * shard_levels(rng, extent, cuts, -0.22, 0.18)
    return jnp.clip(array, -reach, reach).astype(held_as)


def setup_inputs(seed: int = 0) -> dict:
    arg_keys = jax.random.split(jax.random.key(seed), 7)
    return {
        "source": bell_draw(arg_keys[0], (NZ, NR, NT), 1.0, 6.0, ((0, 16), (1, 16)), jnp.float32),
        "pressure_old": bell_draw(arg_keys[1], (NZ, NR, NT), 1.0, 6.0, ((0, 16), (1, 16)), jnp.float32),
        "density": jnp.clip(jnp.exp(math.log(50.0) - 3.912023 * jax.random.uniform(arg_keys[2], (NZ, NR, NT), jnp.float32) ** shard_levels(arg_keys[2], (NZ, NR, NT), ((0, 16), (1, 16)), -0.2, 0.2)), 1.0, 50.0),
        "radial_forward": draw_radial_forward(jax.random.fold_in(arg_keys[6], 71), 0),
        "radial_back": draw_radial_back(jax.random.fold_in(arg_keys[6], 71), 0),
        "radial_eig": draw_radial_eig(jax.random.fold_in(arg_keys[6], 71), 0),
    }


def correction(padded):
    pres = padded[0]
    inv_rho = padded[1]
    mid_p = pres[1:-1, 1:-1]
    mid_w = inv_rho[1:-1, 1:-1]
    others = ((pres[2:, 1:-1], inv_rho[2:, 1:-1]), (pres[:-2, 1:-1], inv_rho[:-2, 1:-1]), (pres[1:-1, 2:], inv_rho[1:-1, 2:]), (pres[1:-1, :-2], inv_rho[1:-1, :-2]), (jnp.roll(mid_p, 1, axis=2), jnp.roll(mid_w, 1, axis=2)), (jnp.roll(mid_p, -1, axis=2), jnp.roll(mid_w, -1, axis=2)))
    total = jnp.zeros_like(mid_p)
    for other_p, other_w in others:
        total = total + (1.0 - 0.5 * (mid_w + other_w)) * (other_p - mid_p)
    return total

def hartley(field):
    spectrum = jnp.fft.fft(field, axis=2)
    return spectrum.real - spectrum.imag

def pivots(theta, index):
    return jnp.exp(-theta) * jnp.expm1(-2.0 * index * theta) / jnp.expm1(-2.0 * (index + 1.0) * theta)

def reference(source, pressure_old, density, radial_forward, radial_back, radial_eig):
    stacked = jnp.stack([pressure_old, 1.0 / density])
    padded = jnp.pad(stacked, ((0, 0), (1, 1), (1, 1), (0, 0)))
    rhs = source + correction(padded)
    hat = hartley(rhs)
    spec = jnp.einsum('ar,zrt->zat', radial_forward, hat, precision=lax.Precision.HIGHEST)
    modes = jnp.arange(NT).astype(jnp.float32)
    mu = 2.0 - 2.0 * jnp.cos(2.0 * jnp.pi * modes / NT)
    half = 0.5 * (radial_eig[:, None] + mu[None, :])
    theta = jnp.log1p(half + jnp.sqrt(half * (2.0 + half)))
    index = jnp.arange(NZ).astype(jnp.float32) + 1.0

    def down_step(carry, row):
        f_row, m = row
        c = pivots(theta, m)
        g = c * (f_row + carry)
        return (g, (g, c))
    zero = jnp.zeros((NR, NT), jnp.float32)
    _, (g_all, c_all) = lax.scan(down_step, zero, (spec, index))

    def up_step(carry, row):
        g_row, c = row
        u = g_row + c * carry
        return (u, u)
    _, u_all = lax.scan(up_step, zero, (g_all, c_all), reverse=True)
    back = jnp.einsum('ra,zat->zrt', radial_back, u_all, precision=lax.Precision.HIGHEST)
    return hartley(back) / NT
```

```python
import functools

import jax
import jax.numpy as jnp
import numpy as np
from jax import lax
from jax.experimental import pallas as pl
from jax.experimental.pallas import tpu as pltpu
from jax.sharding import PartitionSpec as P

MESH = pl.DeviceIdType.MESH
F32, BF16 = jnp.float32, jnp.bfloat16
DEV = 16
ROWS = 48
AZIM = 256
MODES = 768
KW = 16
ZC = 16
CHUNKS = ROWS // ZC
TILES = 12
NT_DIMS = (((1,), (1,)), ((), ()))
NN_DIMS = (((1,), (0,)), ((), ()))


def split(x):
    hi = x.astype(BF16)
    return hi, (x - hi.astype(F32)).astype(BF16)


def dot3(ah, al, bh, bl, dims):
    def dot(a, b):
        return lax.dot_general(a, b, dims, preferred_element_type=F32)

    return dot(ah, bh) + (dot(ah, bl) + dot(al, bh))


def block_transpose(xs):
    lane = lax.broadcasted_iota(jnp.int32, xs[0].shape, 1)
    xs = list(xs)
    for bit in (2, 1, 0):
        step = 1 << bit
        low = (lane & (16 * step)) == 0
        for i in range(8):
            if i & step:
                continue
            a, b = xs[i], xs[i + step]
            if step == 4:
                moved = pltpu.roll(jnp.where(low, b, a), 64, 1)
                xs[i], xs[i + step] = jnp.where(low, a, moved), jnp.where(low, moved, b)
            else:
                xs[i] = jnp.where(low, a, pltpu.roll(b, 16 * step, 1))
                xs[i + step] = jnp.where(low, pltpu.roll(a, 128 - 16 * step, 1), b)
    return xs


def tiles_of(x):
    return [x[8 * (t // 6) : 8 * (t // 6) + 8, 128 * (t % 6) : 128 * (t % 6) + 128] for t in range(TILES)]


def plane_of(tiles):
    return jnp.concatenate(
        [jnp.concatenate(tiles[6 * half : 6 * half + 6], axis=1) for half in range(2)], axis=0
    )


def kernel(
    src_hbm, p_hbm, d_hbm, fwd_hbm, back_hbm, eig_ref, mu_ref, th_ref, tl_ref, out_hbm,
    src, p, h, esend, ehalo, rh, rl, send, recv, xh, xl, spec, pw, mat, mh, ml, uh, ul,
    bsend, brecv, yh, yl, out, cst, gsend, gown, cres, cin,
    load_sem, own_sem, halo_send, halo_recv, gat_send, gat_recv, z_send, z_recv, c_send, c_recv,
    f_send, f_recv, f_own, b_send, b_recv, b_own, r1_send, r1_recv, r2_send, r2_recv, out_sem,
):
    ax, rad = lax.axis_index("axial"), lax.axis_index("radial")
    zz, core = ax // 2, ax % 2
    ry, rx = rad // 4, rad % 4

    def remote(src_ref, dst_ref, send_sem, recv_sem, device):
        return pltpu.make_async_remote_copy(
            src_ref=src_ref, dst_ref=dst_ref, send_sem=send_sem, recv_sem=recv_sem,
            device_id=device, device_id_type=MESH,
        )

    def await_bytes(ref, sem):
        pltpu.make_async_copy(ref, ref, sem).wait()

    def peer(o):
        return ((ry + o // 4) % 4) * 4 + (rx + o % 4) % 4

    loads = [
        pltpu.make_async_copy(p_hbm, p.at[pl.ds(1, ROWS)], load_sem.at[0]),
        pltpu.make_async_copy(d_hbm, h.at[pl.ds(1, ROWS)], load_sem.at[1]),
        pltpu.make_async_copy(src_hbm, src, load_sem.at[2]),
    ]
    for load in loads:
        load.start()
    zeta = zz % 4
    which, chalf = zeta % 2, zeta // 2
    row_at = pl.multiple_of(24 * core, 8)
    col_at = pl.multiple_of(384 * chalf, 128)

    @pl.when(which == 0)
    def _():
        pltpu.make_async_copy(
            fwd_hbm.at[pl.ds(row_at, 24), pl.ds(col_at, 384)],
            mat.at[0, rad, pl.ds(row_at, 24), pl.ds(col_at, 384)], own_sem,
        ).start()

    @pl.when(which == 1)
    def _():
        pltpu.make_async_copy(
            back_hbm.at[pl.ds(row_at, 24), pl.ds(col_at, 384)],
            mat.at[1, rad, pl.ds(row_at, 24), pl.ds(col_at, 384)], own_sem,
        ).start()

    barrier = pltpu.get_barrier_semaphore()

    def greet(o, carry):
        pl.semaphore_signal(barrier, inc=1, device_id=(ax, (rad + o) % DEV), device_id_type=MESH)
        pl.semaphore_signal(barrier, inc=1, device_id=((ax + o) % DEV, rad), device_id_type=MESH)
        return carry

    lax.fori_loop(1, DEV, greet, 0)

    mu = mu_ref[pl.ds(pl.multiple_of(rad * KW, 8), KW), :]
    half = 0.5 * (eig_ref[...] + jnp.concatenate([mu] * 6, axis=1))
    grow = half + jnp.sqrt(half * (2.0 + half))
    theta = jnp.log1p(grow)
    decay = 1.0 / (1.0 + grow)
    rho = grow * decay
    cst[0] = theta
    cst[1] = rho
    pw[0] = jnp.ones((KW, MODES), F32)

    def power(j, kappa):
        now = jnp.exp(-(j.astype(F32) * theta))
        kappa = kappa + now * pw[j - 1]
        pw[j] = now
        return kappa

    kappa = lax.fori_loop(1, ROWS + 1, power, jnp.zeros((KW, MODES), F32))
    cst[2] = kappa
    pl.semaphore_wait(barrier, 2 * (DEV - 1))

    def z_halo(side, what):
        edge, slot, to = (ROWS - 1, 0, ax + 1) if side == 0 else (0, ROWS + 1, ax - 1)
        ref, dst = (p_hbm, p) if what == 0 else (d_hbm, h)
        return remote(
            ref.at[edge], dst.at[slot], halo_send.at[side, what], halo_recv.at[side, what], (to, rad)
        )

    def r_halo(side):
        to = rad + 1 if side == 0 else rad - 1
        return remote(
            esend.at[side], ehalo.at[side], halo_send.at[2, side], halo_recv.at[2, side], (ax, to)
        )

    has_above, has_below = ax < DEV - 1, ax > 0
    has_right, has_left = rad < DEV - 1, rad > 0

    @pl.when(has_above)
    def _():
        z_halo(0, 0).start()
        z_halo(0, 1).start()

    @pl.when(has_below)
    def _():
        z_halo(1, 0).start()
        z_halo(1, 1).start()

    await_bytes(mat.at[0, 0, pl.ds(0, 24), pl.ds(0, 384)], own_sem)

    def piece(s, count):
        return mat.at[which, pl.ds(s, count), pl.ds(row_at, 24), pl.ds(col_at, 384)]

    def gather_send(o, carry):
        remote(piece(rad, 1), piece(rad, 1), gat_send, gat_recv, (ax, peer(o))).start()
        return carry

    lax.fori_loop(1, DEV, gather_send, 0)

    loads[0].wait()
    loads[1].wait()

    def pack(z, carry):
        esend[0, 0, pl.ds(z, 1), :] = p[z + 1, ROWS - 1 : ROWS, :]
        esend[0, 1, pl.ds(z, 1), :] = 0.5 / h[z + 1, ROWS - 1 : ROWS, :]
        esend[1, 0, pl.ds(z, 1), :] = p[z + 1, 0:1, :]
        esend[1, 1, pl.ds(z, 1), :] = 0.5 / h[z + 1, 0:1, :]
        return carry

    lax.fori_loop(0, ROWS, pack, 0)

    @pl.when(has_right)
    def _():
        r_halo(0).start()

    @pl.when(has_left)
    def _():
        r_halo(1).start()

    def weigh(z, carry):
        h[z + 1] = 0.5 / h[z + 1]
        return carry

    lax.fori_loop(0, ROWS, weigh, 0)
    loads[2].wait()

    @pl.when(has_below)
    def _():
        z_halo(0, 0).wait_recv()
        z_halo(0, 1).wait_recv()
        h[0] = 0.5 / h[0]

    @pl.when(jnp.logical_not(has_below))
    def _():
        p[0] = jnp.zeros((ROWS, AZIM), F32)
        h[0] = jnp.zeros((ROWS, AZIM), F32)

    @pl.when(has_above)
    def _():
        z_halo(1, 0).wait_recv()
        z_halo(1, 1).wait_recv()
        h[ROWS + 1] = 0.5 / h[ROWS + 1]

    @pl.when(jnp.logical_not(has_above))
    def _():
        p[ROWS + 1] = jnp.zeros((ROWS, AZIM), F32)
        h[ROWS + 1] = jnp.zeros((ROWS, AZIM), F32)

    @pl.when(has_left)
    def _():
        r_halo(0).wait_recv()

    @pl.when(jnp.logical_not(has_left))
    def _():
        ehalo[0] = jnp.zeros((2, ROWS, AZIM), F32)

    @pl.when(has_right)
    def _():
        r_halo(1).wait_recv()

    @pl.when(jnp.logical_not(has_right))
    def _():
        ehalo[1] = jnp.zeros((2, ROWS, AZIM), F32)

    row = lax.broadcasted_iota(jnp.int32, (ROWS, AZIM), 0)

    def front(c, carry):
        def cells(zl, carry):
            z = c * ZC + zl
            mid_p, mid_h = p[z + 1], h[z + 1]
            base = 1.0 - mid_h

            def term(other_p, other_h):
                return (base - other_h) * (other_p - mid_p)

            def radial(side):
                edge = 0 if side == 0 else ROWS - 1
                shift = 1 if side == 0 else ROWS - 1
                return [
                    jnp.where(row == edge, ehalo[side, i, pl.ds(z, 1), :], pltpu.roll(mid, shift, 0))
                    for i, mid in enumerate((mid_p, mid_h))
                ]

            total = src[z] + term(p[z + 2], h[z + 2]) + term(p[z], h[z])
            total = total + term(*radial(1)) + term(*radial(0))
            total = total + term(pltpu.roll(mid_p, 1, 1), pltpu.roll(mid_h, 1, 1))
            total = total + term(pltpu.roll(mid_p, AZIM - 1, 1), pltpu.roll(mid_h, AZIM - 1, 1))
            hi, lo = split(total)
            for j in range(3):
                at = pl.multiple_of((zl // 8) * 384 + j * 128 + (zl % 8) * 16, 16)
                rh[pl.ds(at, 16), :] = hi[16 * j : 16 * j + 16]
                rl[pl.ds(at, 16), :] = lo[16 * j : 16 * j + 16]
            return carry

        lax.fori_loop(0, ZC, cells, 0)
        for n in range(3):
            cols = pl.ds(256 * n, 256)
            send[c, :, cols] = dot3(th_ref[...], tl_ref[...], rh[cols, :], rl[cols, :], NT_DIMS)

        def ship(o, carry):
            to = peer(o)
            remote(
                send.at[c, pl.ds(pl.multiple_of(to * KW, 8), KW)], recv.at[c, rad],
                f_send.at[c], f_recv.at[c], (ax, to),
            ).start()
            return carry

        lax.fori_loop(1, DEV, ship, 0)
        pltpu.make_async_copy(
            send.at[c, pl.ds(pl.multiple_of(rad * KW, 8), KW)], recv.at[c, rad], f_own.at[c]
        ).start()
        return carry

    lax.fori_loop(0, CHUNKS, front, 0)

    await_bytes(mat.at[0, pl.ds(0, DEV - 1), pl.ds(0, 24), pl.ds(0, 384)], gat_recv)

    def chip(step):
        return ((zz + step) % 8) * 2 + core

    def region(step, s, count):
        z4 = (zz + step + 8) % 4
        return mat.at[
            z4 % 2, pl.ds(s, count), pl.ds(row_at, 24),
            pl.ds(pl.multiple_of(384 * (z4 // 2), 128), 384),
        ]

    hops = ((1, 0, DEV), (7, 0, DEV), (2, 0, DEV // 2), (6, DEV // 2, DEV // 2))
    z_out = [
        remote(region(0, s, n), region(0, s, n), z_send.at[i], z_recv.at[i], (chip(step), rad))
        for i, (step, s, n) in enumerate(hops)
    ]
    for copy in z_out:
        copy.start()
    other = zz * 2 + 1 - core

    def swap(i, step):
        return remote(region(step, 0, DEV), region(step, 0, DEV), c_send.at[i], c_recv.at[i], (other, rad))

    swap(0, 0).start()
    await_bytes(region(0, 0, DEV), z_recv.at[0])
    swap(1, 7).start()
    await_bytes(region(0, 0, DEV), z_recv.at[1])
    swap(2, 1).start()
    await_bytes(region(0, 0, DEV // 2), z_recv.at[2])
    await_bytes(region(0, 0, DEV // 2), z_recv.at[3])
    swap(3, 2).start()
    for i in range(4):
        await_bytes(region(0, 0, DEV), c_recv.at[i])

    def split_mat(s, carry):
        at = pl.ds(pl.multiple_of(s * ROWS, 16), ROWS)
        for i in range(2):
            mh[i, at, :], ml[i, at, :] = split(mat[i, s])
        return carry

    lax.fori_loop(0, DEV, split_mat, 0)

    def middle(c, carry):
        await_bytes(recv.at[0, pl.ds(0, DEV - 1)], f_recv.at[c])
        await_bytes(recv.at[0, 0], f_own.at[c])

        def regroup(hz, carry):
            for v in range(6):
                xs = []
                for e in range(8):
                    s, j = divmod(8 * v + e, 3)
                    xs.append(recv[c, s, :, pl.ds(pl.multiple_of(hz * 384 + j * 128, 128), 128)])
                for zl, y in enumerate(block_transpose(xs)):
                    at = pl.ds(pl.multiple_of(hz * 128 + zl * 16, 16), 16)
                    xh[at, 128 * v : 128 * v + 128], xl[at, 128 * v : 128 * v + 128] = split(y)
            return carry

        lax.fori_loop(0, 2, regroup, 0)
        at = pl.ds(c * ZC, ZC)

        def transform(n, carry):
            rows = pl.ds(pl.multiple_of(256 * n, 256), 256)
            part = dot3(xh[...], xl[...], mh[0, rows, :], ml[0, rows, :], NT_DIMS)
            spec[at, :, rows] = part.reshape(ZC, KW, 256)
            return carry

        lax.fori_loop(0, 3, transform, 0)

        def sweep(zl, carry):
            g, first = carry
            z = c * ZC + zl
            g = spec[z] + g
            g = g - cst[1] * g
            spec[z] = g
            return g, first + pw[z] * g

        return lax.fori_loop(0, ZC, sweep, carry)

    zero = jnp.zeros((KW, MODES), F32)
    last, first = lax.fori_loop(0, CHUNKS, middle, (zero, zero))

    for t, (a, b) in enumerate(zip(tiles_of(last), tiles_of(first))):
        gsend[t, 0] = a
        gsend[t, 1] = b
    is_owner = ax % 4 != 3
    tile = jnp.minimum(ax - ax // 4, TILES - 1)

    def to_owner(t):
        return remote(gsend.at[t], gown.at[ax], r1_send.at[t], r1_recv, (t + t // 3, rad))

    for t in range(TILES):

        @pl.when(ax != t + t // 3)
        def _(t=t):
            to_owner(t).start()

    def to_block(o):
        return remote(cres.at[(ax + o) % DEV], cin.at[tile], r2_send, r2_recv, ((ax + o) % DEV, rad))

    @pl.when(is_owner)
    def _():
        at = (pl.ds(pl.multiple_of(8 * (tile // 6), 8), 8), pl.ds(pl.multiple_of(128 * (tile % 6), 128), 128))
        span = pw[ROWS, at[0], at[1]]
        kap = cst[2, at[0], at[1]]
        th = cst[0, at[0], at[1]]
        await_bytes(gown.at[pl.ds(0, DEV - 1)], r1_recv)
        gown[ax] = gsend[tile]
        enter = jnp.zeros((8, 128), F32)
        for a in range(DEV):
            cres[a, 0] = enter
            enter = gown[a, 0] + span * enter
        enter = jnp.zeros((8, 128), F32)
        for a in range(DEV - 1, -1, -1):
            cres[a, 1] = enter
            enter = gown[a, 1] + kap * cres[a, 0] + span * enter
        ghost = enter * jnp.exp(-th) / (1.0 - jnp.exp(-float(2 * MODES + 2) * th))
        for a in range(DEV):
            cres[a, 2] = ghost

        def back(o, carry):
            to_block(o).start()
            return carry

        lax.fori_loop(1, DEV, back, 0)
        cin[tile] = cres[ax]
        await_bytes(cin.at[pl.ds(0, TILES - 1)], r2_recv)

    @pl.when(jnp.logical_not(is_owner))
    def _():
        await_bytes(cin, r2_recv)

    below = plane_of([cin[t, 0] for t in range(TILES)])
    above = plane_of([cin[t, 1] for t in range(TILES)])
    ghost = plane_of([cin[t, 2] for t in range(TILES)])
    start = (ax * ROWS).astype(F32)
    cst[3] = below
    cst[4] = ghost * jnp.exp(-start * cst[0])
    cst[5] = ghost * jnp.exp(-(float(2 * MODES + 1 - ROWS) - start) * cst[0])

    def lower(i, carry):
        c = CHUNKS - 1 - i

        def sweep(k, u):
            zl = ZC - 1 - k
            z = c * ZC + zl
            up, down = pw[z + 1], pw[ROWS - z]
            u = (spec[z] + up * cst[3]) + (u - cst[1] * u)
            at = pl.ds(pl.multiple_of(zl * KW, 16), KW)
            uh[at, :], ul[at, :] = split(u - cst[4] * up + cst[5] * down)
            return u

        carry = lax.fori_loop(0, ZC, sweep, carry)

        def transform(n, carry):
            rows = pl.ds(pl.multiple_of(256 * n, 256), 256)
            bsend[c, rows, :] = dot3(mh[1, rows, :], ml[1, rows, :], uh[...], ul[...], NT_DIMS)
            return carry

        lax.fori_loop(0, 3, transform, 0)

        def ship(o, carry):
            to = peer(o)
            remote(
                bsend.at[c, pl.ds(pl.multiple_of(to * ROWS, 8), ROWS)], brecv.at[c, rad],
                b_send.at[c], b_recv.at[c], (ax, to),
            ).start()
            return carry

        lax.fori_loop(1, DEV, ship, 0)
        pltpu.make_async_copy(
            bsend.at[c, pl.ds(pl.multiple_of(rad * ROWS, 8), ROWS)], brecv.at[c, rad], b_own.at[c]
        ).start()
        return carry

    lax.fori_loop(0, CHUNKS, lower, above)

    def finish(i, carry):
        c = CHUNKS - 1 - i
        await_bytes(brecv.at[0, pl.ds(0, DEV - 1)], b_recv.at[c])
        await_bytes(brecv.at[0, 0], b_own.at[c])

        def regroup(k, carry):
            hz, rt = k // 3, k % 3
            for dh in range(2):
                xs = [
                    brecv[
                        c, 8 * dh + e, pl.ds(pl.multiple_of(rt * 16, 8), 16),
                        pl.ds(pl.multiple_of(hz * 128, 128), 128),
                    ]
                    for e in range(8)
                ]
                for zl, y in enumerate(block_transpose(xs)):
                    at = pl.ds(pl.multiple_of(hz * 384 + zl * 48 + rt * 16, 16), 16)
                    yh[at, 128 * dh : 128 * dh + 128], yl[at, 128 * dh : 128 * dh + 128] = split(y)
            return carry

        lax.fori_loop(0, 6, regroup, 0)
        for n in range(3):
            rows = pl.ds(256 * n, 256)
            part = dot3(yh[rows, :], yl[rows, :], th_ref[...], tl_ref[...], NN_DIMS)
            out[pl.ds(pl.multiple_of(c * 768 + 256 * n, 256), 256), :] = part * (1.0 / AZIM)
        at = pl.ds(pl.multiple_of(c * 768, 256), 768)
        pltpu.make_async_copy(out.at[at], out_hbm.at[at], out_sem.at[c]).start()
        return carry

    lax.fori_loop(0, CHUNKS, finish, 0)

    @pl.when(has_above)
    def _():
        z_halo(0, 0).wait_send()
        z_halo(0, 1).wait_send()

    @pl.when(has_below)
    def _():
        z_halo(1, 0).wait_send()
        z_halo(1, 1).wait_send()

    @pl.when(has_right)
    def _():
        r_halo(0).wait_send()

    @pl.when(has_left)
    def _():
        r_halo(1).wait_send()

    await_bytes(mat.at[0, pl.ds(0, DEV - 1), pl.ds(0, 24), pl.ds(0, 384)], gat_send)
    for copy in z_out:
        copy.wait_send()
    for i, step in enumerate((0, 7, 1, 2)):
        swap(i, step).wait_send()
    for t in range(TILES):

        @pl.when(ax != t + t // 3)
        def _(t=t):
            to_owner(t).wait_send()

    @pl.when(is_owner)
    def _():
        await_bytes(cres.at[pl.ds(0, DEV - 1)], r2_send)

    def drain(c, carry):
        await_bytes(recv.at[0, pl.ds(0, DEV - 1)], f_send.at[c])
        await_bytes(brecv.at[0, pl.ds(0, DEV - 1)], b_send.at[c])
        at = pl.ds(pl.multiple_of(c * 768, 256), 768)
        pltpu.make_async_copy(out.at[at], out_hbm.at[at], out_sem.at[c]).wait()
        return carry

    lax.fori_loop(0, CHUNKS, drain, 0)


def constants():
    index = np.arange(AZIM)
    angle = 2.0 * np.pi * (index[:, None] * index[None, :] % AZIM) / AZIM
    table = (np.cos(angle) + np.sin(angle)).astype(np.float32)
    hi = table.astype(jnp.bfloat16)
    lo = (table - hi.astype(np.float32)).astype(jnp.bfloat16)
    mu = (2.0 - 2.0 * np.cos(2.0 * np.pi * index / AZIM)).astype(np.float32)
    return hi, lo, np.ascontiguousarray(np.broadcast_to(mu[:, None], (AZIM, 128)))


def body(source, pressure_old, density, radial_forward, radial_back, radial_eig):
    hi, lo, mu = constants()
    anywhere = pl.BlockSpec(memory_space=pl.ANY)
    vmem = pl.BlockSpec(memory_space=pltpu.VMEM)
    dma = pltpu.SemaphoreType.DMA
    result = pl.pallas_call(
        kernel,
        out_shape=jax.ShapeDtypeStruct((ROWS * ROWS, AZIM), F32),
        in_specs=[anywhere] * 5 + [vmem] * 4,
        out_specs=anywhere,
        scratch_shapes=[
            pltpu.VMEM((ROWS, ROWS, AZIM), F32),
            pltpu.VMEM((ROWS + 2, ROWS, AZIM), F32),
            pltpu.VMEM((ROWS + 2, ROWS, AZIM), F32),
            pltpu.VMEM((2, 2, ROWS, AZIM), F32),
            pltpu.VMEM((2, 2, ROWS, AZIM), F32),
            pltpu.VMEM((ZC * ROWS, AZIM), BF16),
            pltpu.VMEM((ZC * ROWS, AZIM), BF16),
            pltpu.VMEM((CHUNKS, AZIM, ZC * ROWS), F32),
            pltpu.VMEM((CHUNKS, DEV, KW, ZC * ROWS), F32),
            pltpu.VMEM((ZC * KW, MODES), BF16),
            pltpu.VMEM((ZC * KW, MODES), BF16),
            pltpu.VMEM((ROWS, KW, MODES), F32),
            pltpu.VMEM((ROWS + 1, KW, MODES), F32),
            pltpu.VMEM((2, DEV, ROWS, MODES), F32),
            pltpu.VMEM((2, MODES, MODES), BF16),
            pltpu.VMEM((2, MODES, MODES), BF16),
            pltpu.VMEM((ZC * KW, MODES), BF16),
            pltpu.VMEM((ZC * KW, MODES), BF16),
            pltpu.VMEM((CHUNKS, MODES, ZC * KW), F32),
            pltpu.VMEM((CHUNKS, DEV, ROWS, ZC * KW), F32),
            pltpu.VMEM((ZC * ROWS, AZIM), BF16),
            pltpu.VMEM((ZC * ROWS, AZIM), BF16),
            pltpu.VMEM((ROWS * ROWS, AZIM), F32),
            pltpu.VMEM((6, KW, MODES), F32),
            pltpu.VMEM((TILES, 2, 8, 128), F32),
            pltpu.VMEM((DEV, 2, 8, 128), F32),
            pltpu.VMEM((DEV, 3, 8, 128), F32),
            pltpu.VMEM((TILES, 3, 8, 128), F32),
            dma((3,)), dma, dma((3, 2)), dma((3, 2)), dma, dma, dma((4,)), dma((4,)),
            dma((4,)), dma((4,)), dma((CHUNKS,)), dma((CHUNKS,)), dma((CHUNKS,)),
            dma((CHUNKS,)), dma((CHUNKS,)), dma((CHUNKS,)), dma((TILES,)), dma, dma, dma,
            dma((CHUNKS,)),
        ],
        compiler_params=pltpu.CompilerParams(
            collective_id=0, has_side_effects=True, vmem_limit_bytes=60 * 1024 * 1024
        ),
    )(
        source, pressure_old, density, radial_forward, radial_back,
        radial_eig.reshape(1, MODES), jnp.asarray(mu), jnp.asarray(hi), jnp.asarray(lo),
    )
    return result.reshape(ROWS, ROWS, AZIM)


def solution(mesh):
    in_specs = (
        P("axial", "radial", None),
        P("axial", "radial", None),
        P("axial", "radial", None),
        P("radial", None),
        P("radial", None),
        P(),
    )
    out_specs = P("axial", "radial", None)
    return jax.shard_map(body, mesh=mesh, in_specs=in_specs, out_specs=out_specs, check_vma=False)
```

```python
import functools

import jax
import jax.numpy as jnp
import numpy as np
from jax import lax
from jax.experimental import pallas as pl
from jax.experimental.pallas import tpu as pltpu
from jax.sharding import PartitionSpec as P

MESH = pl.DeviceIdType.MESH
F32, BF16 = jnp.float32, jnp.bfloat16
DEV = 16
ROWS = 48
AZIM = 256
MODES = 768
KW = 8
ZC = 16
CHUNKS = ROWS // ZC
TILES = 6
UNIT = ZC * ROWS
OFFSETS = (
    (0, 1), (0, 3), (1, 0), (3, 0), (1, 1), (3, 3), (1, 3), (3, 1), (0, 2), (2, 0), (2, 2), (1, 2), (3, 2), (2, 1), (2, 3),
)
NT_DIMS = (((1,), (1,)), ((), ()))
NN_DIMS = (((1,), (0,)), ((), ()))


def split(x):
    hi = x.astype(BF16)
    return hi, (x - hi.astype(F32)).astype(BF16)


def dot3(ah, al, bh, bl, dims):
    def dot(a, b):
        return lax.dot_general(a, b, dims, preferred_element_type=F32)

    return dot(ah, bh) + (dot(ah, bl) + dot(al, bh))


def block_transpose(xs, width):
    lane = lax.broadcasted_iota(jnp.int32, xs[0].shape, 1)
    xs = list(xs)
    step = len(xs) // 2
    while step:
        shift = width * step
        low = (lane & shift) == 0
        for i in range(len(xs)):
            if i & step:
                continue
            a, b = xs[i], xs[i + step]
            if shift == 64:
                moved = pltpu.roll(jnp.where(low, b, a), 64, 1)
                xs[i], xs[i + step] = jnp.where(low, a, moved), jnp.where(low, moved, b)
            else:
                xs[i] = jnp.where(low, a, pltpu.roll(b, shift, 1))
                xs[i + step] = jnp.where(low, pltpu.roll(a, 128 - shift, 1), b)
        step //= 2
    return xs


def tiles_of(x):
    return [x[:, 128 * t : 128 * t + 128] for t in range(TILES)]


def kernel(
    src_hbm, p_hbm, d_hbm, fwd_hbm, back_hbm, eig_ref, mu_ref, th_ref, tl_ref, out_hbm,
    src, p, h, esend, ehalo, rh, rl, send, recv, xh, xl, spec, pw, mat, mh, ml, uh, ul,
    bsend, brecv, yh, yl, out, cst, gsend, gown, cres, cin,
    load_sem, own_sem, halo_send, halo_recv, gat_send, gat_recv, z_send, z_recv, c_send, c_recv,
    f_send, f_recv, f_own, b_send, b_recv, b_own, r1_send, r1_recv, r2_send, r2_recv, out_sem,
):
    ax, rad = lax.axis_index("axial"), lax.axis_index("radial")
    zz, core = ax // 2, ax % 2
    ry, rx = rad // 4, rad % 4

    def remote(src_ref, dst_ref, send_sem, recv_sem, device):
        return pltpu.make_async_remote_copy(
            src_ref=src_ref, dst_ref=dst_ref, send_sem=send_sem, recv_sem=recv_sem,
            device_id=device, device_id_type=MESH,
        )

    def await_bytes(ref, sem):
        pltpu.make_async_copy(ref, ref, sem).wait()

    def peers():
        for a, b in OFFSETS:
            yield ((ry + a + core * (b - a)) % 4) * 4 + (rx + b + core * (a - b)) % 4

    loads = [
        pltpu.make_async_copy(p_hbm, p.at[pl.ds(1, ROWS)], load_sem.at[0]),
        pltpu.make_async_copy(d_hbm, h.at[pl.ds(1, ROWS)], load_sem.at[1]),
        pltpu.make_async_copy(src_hbm, src, load_sem.at[2]),
    ]
    for load in loads:
        load.start()
    zeta = zz % 4
    which, chalf = zeta % 2, zeta // 2
    row_at = pl.multiple_of(24 * core, 8)
    col_at = pl.multiple_of(384 * chalf, 128)
    holds_fwd, holds_back = which == 0, which == 1

    for i, (mine, ref) in enumerate(((holds_fwd, fwd_hbm), (holds_back, back_hbm))):

        @pl.when(mine)
        def _(i=i, ref=ref):
            pltpu.make_async_copy(
                ref.at[pl.ds(row_at, 24), pl.ds(col_at, 384)],
                mat.at[i, rad, pl.ds(row_at, 24), pl.ds(col_at, 384)], own_sem,
            ).start()

    barrier = pltpu.get_barrier_semaphore()

    def greet(o, carry):
        pl.semaphore_signal(barrier, inc=1, device_id=(ax, (rad + o) % DEV), device_id_type=MESH)
        pl.semaphore_signal(barrier, inc=1, device_id=((ax + o) % DEV, rad), device_id_type=MESH)
        return carry

    lax.fori_loop(1, DEV, greet, 0)

    loads[0].wait()
    loads[1].wait()

    def pack(z, carry):
        esend[0, 0, pl.ds(z, 1), :] = p[z + 1, ROWS - 1 : ROWS, :]
        esend[0, 1, pl.ds(z, 1), :] = 0.5 / h[z + 1, ROWS - 1 : ROWS, :]
        esend[1, 0, pl.ds(z, 1), :] = p[z + 1, 0:1, :]
        esend[1, 1, pl.ds(z, 1), :] = 0.5 / h[z + 1, 0:1, :]
        return carry

    lax.fori_loop(0, ROWS, pack, 0)

    pl.semaphore_wait(barrier, 2 * (DEV - 1))

    def z_halo(side, what):
        edge, slot, to = (ROWS - 1, 0, ax + 1) if side == 0 else (0, ROWS + 1, ax - 1)
        ref, dst = (p_hbm, p) if what == 0 else (d_hbm, h)
        return remote(
            ref.at[edge], dst.at[slot], halo_send.at[side, what], halo_recv.at[side, what], (to, rad)
        )

    def r_halo(side):
        to = rad + 1 if side == 0 else rad - 1
        return remote(
            esend.at[side], ehalo.at[side], halo_send.at[2, side], halo_recv.at[2, side], (ax, to)
        )

    has_above, has_below = ax < DEV - 1, ax > 0
    has_right, has_left = rad < DEV - 1, rad > 0

    @pl.when(has_right)
    def _():
        r_halo(0).start()

    @pl.when(has_left)
    def _():
        r_halo(1).start()

    @pl.when(has_above)
    def _():
        z_halo(0, 0).start()
        z_halo(0, 1).start()

    @pl.when(has_below)
    def _():
        z_halo(1, 0).start()
        z_halo(1, 1).start()

    await_bytes(mat.at[0, 0, pl.ds(0, 24), pl.ds(0, 384)], own_sem)
    piece = mat.at[which, rad, pl.ds(row_at, 24), pl.ds(col_at, 384)]
    for to in peers():
        remote(piece, piece, gat_send, gat_recv, (ax, to)).start()

    def weigh(z, carry):
        h[z + 1] = 0.5 / h[z + 1]
        return carry

    lax.fori_loop(0, ROWS, weigh, 0)
    for kh in range(2):
        mu = mu_ref[pl.ds(pl.multiple_of(rad * 2 * KW + kh * KW, 8), KW), :]
        half = 0.5 * (eig_ref[...].reshape(1, MODES) + jnp.concatenate([mu] * TILES, axis=1))
        grow = half + jnp.sqrt(half * (2.0 + half))
        theta = jnp.log1p(grow)
        cst[kh, 0] = theta
        cst[kh, 1] = grow / (1.0 + grow)
        pw[kh, 0] = jnp.ones((KW, MODES), F32)

        def power(j, kappa, kh=kh, theta=theta):
            now = jnp.exp(-(j.astype(F32) * theta))
            kappa = kappa + now * pw[kh, j - 1]
            pw[kh, j] = now
            return kappa

        cst[kh, 2] = lax.fori_loop(1, ROWS + 1, power, jnp.zeros((KW, MODES), F32))

    loads[2].wait()

    @pl.when(has_below)
    def _():
        z_halo(0, 0).wait_recv()
        z_halo(0, 1).wait_recv()
        h[0] = 0.5 / h[0]

    @pl.when(jnp.logical_not(has_below))
    def _():
        p[0] = jnp.zeros((ROWS, AZIM), F32)
        h[0] = jnp.zeros((ROWS, AZIM), F32)

    @pl.when(has_above)
    def _():
        z_halo(1, 0).wait_recv()
        z_halo(1, 1).wait_recv()
        h[ROWS + 1] = 0.5 / h[ROWS + 1]

    @pl.when(jnp.logical_not(has_above))
    def _():
        p[ROWS + 1] = jnp.zeros((ROWS, AZIM), F32)
        h[ROWS + 1] = jnp.zeros((ROWS, AZIM), F32)

    @pl.when(has_left)
    def _():
        r_halo(0).wait_recv()

    @pl.when(jnp.logical_not(has_left))
    def _():
        ehalo[0] = jnp.zeros((2, ROWS, AZIM), F32)

    @pl.when(has_right)
    def _():
        r_halo(1).wait_recv()

    @pl.when(jnp.logical_not(has_right))
    def _():
        ehalo[1] = jnp.zeros((2, ROWS, AZIM), F32)

    def chip(step):
        return ((zz + step) % 8) * 2 + core

    def region(step, s, count):
        z4 = (zz + step) % 4
        return mat.at[
            z4 % 2, pl.ds(s, count), pl.ds(row_at, 24),
            pl.ds(pl.multiple_of(384 * (z4 // 2), 128), 384),
        ]

    z_out = [
        remote(region(0, s, n), region(0, s, n), z_send.at[i], z_recv.at[i], (chip(step), rad))
        for i, (step, s, n) in enumerate(
            ((1, 0, DEV), (7, 0, DEV), (2, 0, DEV // 2), (6, DEV // 2, DEV // 2))
        )
    ]

    def swap(i):
        step = (0, 7, 1, 2)[i]
        return remote(
            region(step, 0, DEV), region(step, 0, DEV), c_send.at[i], c_recv.at[i],
            (zz * 2 + 1 - core, rad),
        )

    def pass_on():
        for i in (2, 3, 0, 1):
            z_out[i].start()
        swap(0).start()

    def pass_beside():
        for i in range(2):
            await_bytes(region(0, 0, DEV), z_recv.at[i])
            swap(1 + i).start()

    def pass_across():
        for i in (2, 3):
            await_bytes(region(0, 0, DEV // 2), z_recv.at[i])
        swap(3).start()

    def arrived(*steps):
        for i in steps:
            await_bytes(region(0, 0, DEV), c_recv.at[i])

    def split_mat(i):
        def one(s, carry):
            at = pl.ds(pl.multiple_of(s * ROWS, 16), ROWS)
            mh[i, at, :], ml[i, at, :] = split(mat[i, s])
            return carry

        lax.fori_loop(0, DEV, one, 0)

    row = lax.broadcasted_iota(jnp.int32, (ROWS, AZIM), 0)

    def ship_in(kh, c):
        for to in peers():
            remote(
                send.at[c, pl.ds(pl.multiple_of(kh * 128 + to * KW, 8), KW)], recv.at[kh, c, rad],
                f_send.at[kh, c], f_recv.at[kh, c], (ax, to),
            ).start()
        pltpu.make_async_copy(
            send.at[c, pl.ds(pl.multiple_of(kh * 128 + rad * KW, 8), KW)], recv.at[kh, c, rad],
            f_own.at[kh, c],
        ).start()

    def front(c, carry):
        def cells(zl, carry):
            z = c * ZC + zl
            mid_p, mid_h = p[z + 1], h[z + 1]
            base = 1.0 - mid_h

            def term(other_p, other_h):
                return (base - other_h) * (other_p - mid_p)

            def radial(side):
                edge = 0 if side == 0 else ROWS - 1
                shift = 1 if side == 0 else ROWS - 1
                return [
                    jnp.where(row == edge, ehalo[side, i, pl.ds(z, 1), :], pltpu.roll(mid, shift, 0))
                    for i, mid in enumerate((mid_p, mid_h))
                ]

            total = src[z] + term(p[z + 2], h[z + 2]) + term(p[z], h[z])
            total = total + term(*radial(1)) + term(*radial(0))
            total = total + term(pltpu.roll(mid_p, 1, 1), pltpu.roll(mid_h, 1, 1))
            total = total + term(pltpu.roll(mid_p, AZIM - 1, 1), pltpu.roll(mid_h, AZIM - 1, 1))
            hi, lo = split(total)
            for j in range(3):
                at = pl.multiple_of((zl // 8) * 384 + j * 128 + (zl % 8) * 16, 16)
                rh[pl.ds(at, 16), :] = hi[16 * j : 16 * j + 16]
                rl[pl.ds(at, 16), :] = lo[16 * j : 16 * j + 16]
            return carry

        lax.fori_loop(0, ZC, cells, 0)
        for n in range(3):
            cols = pl.ds(256 * n, 256)
            send[c, :, cols] = dot3(th_ref[...], tl_ref[...], rh[cols, :], rl[cols, :], NT_DIMS)
        ship_in(0, c)

        @pl.when(c == 0)
        def _():
            await_bytes(mat.at[0, pl.ds(0, DEV - 1), pl.ds(0, 24), pl.ds(0, 384)], gat_recv)
            pl.when(holds_fwd)(pass_on)

        return carry

    lax.fori_loop(0, CHUNKS, front, 0)

    def second_half(c, carry):
        ship_in(1, c)
        return carry

    lax.fori_loop(0, CHUNKS, second_half, 0)
    pl.when(holds_back)(pass_on)
    pl.when(holds_fwd)(pass_across)
    pl.when(holds_back)(pass_beside)

    def regroup_in(kh, c):
        await_bytes(recv.at[0, 0, pl.ds(0, DEV - 1)], f_recv.at[kh, c])
        await_bytes(recv.at[0, 0, 0], f_own.at[kh, c])

        def one(hz, carry):
            for v in range(TILES):
                xs = []
                for e in range(8):
                    s, j = divmod(8 * v + e, 3)
                    xs.append(recv[kh, c, s, :, pl.ds(pl.multiple_of(hz * 384 + j * 128, 128), 128)])
                ys = block_transpose(xs, 16)
                for i in range(4):
                    at = pl.ds(pl.multiple_of(c * 128 + hz * 64 + i * 16, 16), 16)
                    y = jnp.concatenate(ys[2 * i : 2 * i + 2], axis=0)
                    xh[at, 128 * v : 128 * v + 128], xl[at, 128 * v : 128 * v + 128] = split(y)
            return carry

        lax.fori_loop(0, 2, one, 0)

    def to_owner(kh, t):
        tile = kh * TILES + t
        return remote(
            gsend.at[kh, t], gown.at[ax], r1_send.at[kh, t], r1_recv, (tile + tile // 3, rad)
        )

    def each_owner(kh, act):
        for t in range(TILES):
            tile = kh * TILES + t

            @pl.when(ax != tile + tile // 3)
            def _(t=t):
                act(to_owner(kh, t))

    def upward(kh):
        def transform(n, carry):
            rows = pl.ds(pl.multiple_of(256 * n, 256), 256)
            part = dot3(xh[...], xl[...], mh[0, rows, :], ml[0, rows, :], NT_DIMS)
            spec[kh, :, :, rows] = part.reshape(ROWS, KW, 256)
            return carry

        lax.fori_loop(0, 3, transform, 0)

        def sweep(z, carry):
            g, first = carry
            g = spec[kh, z] + g
            g = g - cst[kh, 1] * g
            spec[kh, z] = g
            return g, first + pw[kh, z] * g

        zero = jnp.zeros((KW, MODES), F32)
        last, first = lax.fori_loop(0, ROWS, sweep, (zero, zero))
        for t, (a, b) in enumerate(zip(tiles_of(last), tiles_of(first))):
            gsend[kh, t, 0] = a
            gsend[kh, t, 1] = b
        each_owner(kh, lambda copy: copy.start())

    tile = jnp.minimum(ax - ax // 4, 2 * TILES - 1)
    my_half, my_tile = tile // TILES, tile % TILES
    is_owner = ax % 4 != 3

    def to_block(kh, o):
        to = (ax + o) % DEV
        return remote(cres.at[to], cin.at[kh, my_tile], r2_send, r2_recv.at[kh], (to, rad))

    def owner(kh):
        @pl.when(is_owner & (my_half == kh))
        def _():
            lanes = pl.ds(pl.multiple_of(128 * my_tile, 128), 128)
            span = pw[kh, ROWS, :, lanes]
            kap = cst[kh, 2, :, lanes]
            th = cst[kh, 0, :, lanes]
            await_bytes(gown.at[pl.ds(0, DEV - 1)], r1_recv)
            gown[ax] = gsend[kh, my_tile]
            enter = jnp.zeros((8, 128), F32)
            for a in range(DEV):
                cres[a, 0] = enter
                enter = gown[a, 0] + span * enter
            enter = jnp.zeros((8, 128), F32)
            for a in range(DEV - 1, -1, -1):
                cres[a, 1] = enter
                enter = gown[a, 1] + kap * cres[a, 0] + span * enter
            ghost = enter * jnp.exp(-th) / (1.0 - jnp.exp(-float(2 * MODES + 2) * th))
            for a in range(DEV):
                cres[a, 2] = ghost

            def back(o, carry):
                to_block(kh, o).start()
                return carry

            lax.fori_loop(1, DEV, back, 0)
            cin[kh, my_tile] = cres[ax]

    def downward(kh):
        @pl.when(is_owner & (my_half == kh))
        def _():
            await_bytes(cin.at[kh, pl.ds(0, TILES - 1)], r2_recv.at[kh])

        @pl.when(jnp.logical_not(is_owner & (my_half == kh)))
        def _():
            await_bytes(cin.at[kh], r2_recv.at[kh])

        below, above, ghost = [
            jnp.concatenate([cin[kh, t, i] for t in range(TILES)], axis=1) for i in range(3)
        ]
        start = (ax * ROWS).astype(F32)
        cst[kh, 3] = below
        cst[kh, 4] = ghost * jnp.exp(-start * cst[kh, 0])
        cst[kh, 5] = ghost * jnp.exp(-(float(2 * MODES + 1 - ROWS) - start) * cst[kh, 0])

        def lower(i, carry):
            c = CHUNKS - 1 - i

            def sweep(k, u):
                pair = ZC // 2 - 1 - k
                res = [None, None]
                for q in (1, 0):
                    z = c * ZC + 2 * pair + q
                    up, down = pw[kh, z + 1], pw[kh, ROWS - z]
                    u = (spec[kh, z] + up * cst[kh, 3]) + (u - cst[kh, 1] * u)
                    res[q] = u - cst[kh, 4] * up + cst[kh, 5] * down
                at = pl.ds(pl.multiple_of(pair * 2 * KW, 16), 2 * KW)
                uh[at, :], ul[at, :] = split(jnp.concatenate(res, axis=0))
                return u

            carry = lax.fori_loop(0, ZC // 2, sweep, carry)

            def transform(n, carry):
                rows = pl.ds(pl.multiple_of(256 * n, 256), 256)
                bsend[kh, c, rows, :] = dot3(mh[1, rows, :], ml[1, rows, :], uh[...], ul[...], NT_DIMS)
                return carry

            lax.fori_loop(0, 3, transform, 0)
            for to in peers():
                remote(
                    bsend.at[kh, c, pl.ds(pl.multiple_of(to * ROWS, 8), ROWS)], brecv.at[kh, c, rad],
                    b_send.at[kh, c], b_recv.at[kh, c], (ax, to),
                ).start()
            pltpu.make_async_copy(
                bsend.at[kh, c, pl.ds(pl.multiple_of(rad * ROWS, 8), ROWS)], brecv.at[kh, c, rad],
                b_own.at[kh, c],
            ).start()
            return carry

        lax.fori_loop(0, CHUNKS, lower, above)

    pl.when(holds_fwd)(lambda: arrived(0, 3))
    pl.when(holds_back)(lambda: arrived(1, 2))
    split_mat(0)
    for c in range(CHUNKS):
        regroup_in(0, c)
    upward(0)
    regroup_in(1, 0)
    owner(0)
    pl.when(holds_fwd)(pass_beside)
    pl.when(holds_back)(pass_across)
    regroup_in(1, 1)
    pl.when(holds_fwd)(lambda: arrived(1, 2))
    pl.when(holds_back)(lambda: arrived(0, 3))
    split_mat(1)
    downward(0)
    regroup_in(1, 2)
    upward(1)
    owner(1)
    downward(1)

    def regroup_out(kh, c):
        await_bytes(brecv.at[0, 0, pl.ds(0, DEV - 1)], b_recv.at[kh, c])
        await_bytes(brecv.at[0, 0, 0], b_own.at[kh, c])

        def one(rt, carry):
            xs = [brecv[kh, c, d, pl.ds(pl.multiple_of(rt * 16, 8), 16), :] for d in range(DEV)]
            for zl, y in enumerate(block_transpose(xs, 8)):
                at = pl.ds(pl.multiple_of(c * UNIT + zl * ROWS + rt * 16, 16), 16)
                yh[at, 128 * kh : 128 * kh + 128], yl[at, 128 * kh : 128 * kh + 128] = split(y)
            return carry

        lax.fori_loop(0, 3, one, 0)

    def early(i, carry):
        regroup_out(0, CHUNKS - 1 - i)
        return carry

    lax.fori_loop(0, CHUNKS, early, 0)

    def finish(i, carry):
        c = CHUNKS - 1 - i
        regroup_out(1, c)

        def transform(n, carry):
            rows = pl.ds(pl.multiple_of(c * UNIT + 256 * n, 256), 256)
            part = dot3(yh[rows, :], yl[rows, :], th_ref[...], tl_ref[...], NN_DIMS)
            out[rows, :] = part * (1.0 / AZIM)
            return carry

        lax.fori_loop(0, 3, transform, 0)
        at = pl.ds(pl.multiple_of(c * UNIT, 256), UNIT)
        pltpu.make_async_copy(out.at[at], out_hbm.at[at], out_sem.at[c]).start()
        return carry

    lax.fori_loop(0, CHUNKS, finish, 0)

    @pl.when(has_above)
    def _():
        z_halo(0, 0).wait_send()
        z_halo(0, 1).wait_send()

    @pl.when(has_below)
    def _():
        z_halo(1, 0).wait_send()
        z_halo(1, 1).wait_send()

    @pl.when(has_right)
    def _():
        r_halo(0).wait_send()

    @pl.when(has_left)
    def _():
        r_halo(1).wait_send()

    await_bytes(mat.at[0, pl.ds(0, DEV - 1), pl.ds(0, 24), pl.ds(0, 384)], gat_send)
    for copy in z_out:
        copy.wait_send()
    for i in range(4):
        swap(i).wait_send()
    for kh in range(2):
        each_owner(kh, lambda copy: copy.wait_send())

    @pl.when(is_owner)
    def _():
        await_bytes(cres.at[pl.ds(0, DEV - 1)], r2_send)

    def drain(c, carry):
        for kh in range(2):
            await_bytes(recv.at[0, 0, pl.ds(0, DEV - 1)], f_send.at[kh, c])
            await_bytes(brecv.at[0, 0, pl.ds(0, DEV - 1)], b_send.at[kh, c])
        at = pl.ds(pl.multiple_of(c * UNIT, 256), UNIT)
        pltpu.make_async_copy(out.at[at], out_hbm.at[at], out_sem.at[c]).wait()
        return carry

    lax.fori_loop(0, CHUNKS, drain, 0)


def constants():
    index = np.arange(AZIM)
    angle = 2.0 * np.pi * (index[:, None] * index[None, :] % AZIM) / AZIM
    table = (np.cos(angle) + np.sin(angle)).astype(np.float32)
    hi = table.astype(jnp.bfloat16)
    lo = (table - hi.astype(np.float32)).astype(jnp.bfloat16)
    order = np.arange(AZIM).reshape(DEV, 2, KW).transpose(1, 0, 2).reshape(-1)
    hi, lo = hi[order], lo[order]
    mu = (2.0 - 2.0 * np.cos(2.0 * np.pi * index / AZIM)).astype(np.float32)
    return hi, lo, np.ascontiguousarray(np.broadcast_to(mu[:, None], (AZIM, 128)))


def body(source, pressure_old, density, radial_forward, radial_back, radial_eig):
    hi, lo, mu = constants()
    anywhere = pl.BlockSpec(memory_space=pl.ANY)
    vmem = pl.BlockSpec(memory_space=pltpu.VMEM)
    dma = pltpu.SemaphoreType.DMA
    result = pl.pallas_call(
        kernel,
        out_shape=jax.ShapeDtypeStruct((ROWS * ROWS, AZIM), F32),
        in_specs=[anywhere] * 5 + [vmem] * 4,
        out_specs=anywhere,
        scratch_shapes=[
            pltpu.VMEM((ROWS, ROWS, AZIM), F32),
            pltpu.VMEM((ROWS + 2, ROWS, AZIM), F32),
            pltpu.VMEM((ROWS + 2, ROWS, AZIM), F32),
            pltpu.VMEM((2, 2, ROWS, AZIM), F32),
            pltpu.VMEM((2, 2, ROWS, AZIM), F32),
            pltpu.VMEM((UNIT, AZIM), BF16),
            pltpu.VMEM((UNIT, AZIM), BF16),
            pltpu.VMEM((CHUNKS, AZIM, UNIT), F32),
            pltpu.VMEM((2, CHUNKS, DEV, KW, UNIT), F32),
            pltpu.VMEM((ROWS * KW, MODES), BF16),
            pltpu.VMEM((ROWS * KW, MODES), BF16),
            pltpu.VMEM((2, ROWS, KW, MODES), F32),
            pltpu.VMEM((2, ROWS + 1, KW, MODES), F32),
            pltpu.VMEM((2, DEV, ROWS, MODES), F32),
            pltpu.VMEM((2, MODES, MODES), BF16),
            pltpu.VMEM((2, MODES, MODES), BF16),
            pltpu.VMEM((ZC * KW, MODES), BF16),
            pltpu.VMEM((ZC * KW, MODES), BF16),
            pltpu.VMEM((2, CHUNKS, MODES, ZC * KW), F32),
            pltpu.VMEM((2, CHUNKS, DEV, ROWS, ZC * KW), F32),
            pltpu.VMEM((ROWS * ROWS, AZIM), BF16),
            pltpu.VMEM((ROWS * ROWS, AZIM), BF16),
            pltpu.VMEM((ROWS * ROWS, AZIM), F32),
            pltpu.VMEM((2, 6, KW, MODES), F32),
            pltpu.VMEM((2, TILES, 2, 8, 128), F32),
            pltpu.VMEM((DEV, 2, 8, 128), F32),
            pltpu.VMEM((DEV, 3, 8, 128), F32),
            pltpu.VMEM((2, TILES, 3, 8, 128), F32),
            dma((3,)), dma, dma((3, 2)), dma((3, 2)), dma, dma, dma((4,)), dma((4,)),
            dma((4,)), dma((4,)), dma((2, CHUNKS)), dma((2, CHUNKS)), dma((2, CHUNKS)),
            dma((2, CHUNKS)), dma((2, CHUNKS)), dma((2, CHUNKS)), dma((2, TILES)), dma, dma,
            dma((2,)), dma((CHUNKS,)),
        ],
        compiler_params=pltpu.CompilerParams(
            collective_id=0, has_side_effects=True, vmem_limit_bytes=60 * 1024 * 1024
        ),
    )(
        source, pressure_old, density, radial_forward, radial_back,
        radial_eig, jnp.asarray(mu), jnp.asarray(hi), jnp.asarray(lo),
    )
    return result.reshape(ROWS, ROWS, AZIM)


def solution(mesh):
    in_specs = (
        P("axial", "radial", None),
        P("axial", "radial", None),
        P("axial", "radial", None),
        P("radial", None),
        P("radial", None),
        P(),
    )
    out_specs = P("axial", "radial", None)
    return jax.shard_map(body, mesh=mesh, in_specs=in_specs, out_specs=out_specs, check_vma=False)
```

```python
import functools

import jax
import jax.numpy as jnp
import numpy as np
from jax import lax
from jax.experimental import pallas as pl
from jax.experimental.pallas import tpu as pltpu
from jax.sharding import PartitionSpec as P

MESH = pl.DeviceIdType.MESH
F32, BF16 = jnp.float32, jnp.bfloat16
DEV = 16
ROWS = 48
AZIM = 256
MODES = 768
KW = 8
ZC = 16
CHUNKS = ROWS // ZC
TILES = 6
UNIT = ZC * ROWS
OFFSETS = (
    (0, 1), (0, 3), (1, 0), (3, 0), (1, 1), (3, 3), (1, 3), (3, 1), (0, 2), (2, 0), (2, 2), (1, 2), (3, 2), (2, 1), (2, 3),
)
NT_DIMS = (((1,), (1,)), ((), ()))
NN_DIMS = (((1,), (0,)), ((), ()))


def split(x):
    hi = x.astype(BF16)
    return hi, (x - hi.astype(F32)).astype(BF16)


def dot3(ah, al, bh, bl, dims):
    def dot(a, b):
        return lax.dot_general(a, b, dims, preferred_element_type=F32)

    return dot(ah, bh) + (dot(ah, bl) + dot(al, bh))


def block_transpose(xs, width):
    lane = lax.broadcasted_iota(jnp.int32, xs[0].shape, 1)
    xs = list(xs)
    step = len(xs) // 2
    while step:
        shift = width * step
        low = (lane & shift) == 0
        for i in range(len(xs)):
            if i & step:
                continue
            a, b = xs[i], xs[i + step]
            if shift == 64:
                moved = pltpu.roll(jnp.where(low, b, a), 64, 1)
                xs[i], xs[i + step] = jnp.where(low, a, moved), jnp.where(low, moved, b)
            else:
                xs[i] = jnp.where(low, a, pltpu.roll(b, shift, 1))
                xs[i + step] = jnp.where(low, pltpu.roll(a, 128 - shift, 1), b)
        step //= 2
    return xs


def tiles_of(x):
    return [x[:, 128 * t : 128 * t + 128] for t in range(TILES)]


def kernel(
    src_hbm, p_hbm, d_hbm, fwd_hbm, back_hbm, eig_ref, mu_ref, th_ref, tl_ref, out_hbm,
    src, p, h, esend, ehalo, rh, rl, send, recv, xh, xl, spec, pw, mat, mh, ml, uu,
    bsend, brecv, yh, yl, out, cst, state, gsend, gown, cres, cin,
    load_sem, own_sem, halo_send, halo_recv, gat_send, gat_recv, z_send, z_recv, c_send, c_recv,
    f_send, f_recv, f_own, b_send, b_recv, b_own, r1_send, r1_recv, r2_send, r2_recv, out_sem,
):
    ax, rad = lax.axis_index("axial"), lax.axis_index("radial")
    zz, core = ax // 2, ax % 2
    ry, rx = rad // 4, rad % 4

    def remote(src_ref, dst_ref, send_sem, recv_sem, device):
        return pltpu.make_async_remote_copy(
            src_ref=src_ref, dst_ref=dst_ref, send_sem=send_sem, recv_sem=recv_sem,
            device_id=device, device_id_type=MESH,
        )

    def await_bytes(ref, sem):
        pltpu.make_async_copy(ref, ref, sem).wait()

    def peers():
        for a, b in OFFSETS:
            yield ((ry + a + core * (b - a)) % 4) * 4 + (rx + b + core * (a - b)) % 4

    loads = [
        pltpu.make_async_copy(p_hbm, p.at[pl.ds(1, ROWS)], load_sem.at[0]),
        pltpu.make_async_copy(d_hbm, h.at[pl.ds(1, ROWS)], load_sem.at[1]),
        pltpu.make_async_copy(src_hbm, src, load_sem.at[2]),
    ]
    for load in loads:
        load.start()
    parity = (ry + rx) % 2
    slot = parity * 8 + ry * 2 + rx // 2
    chalf, shalf = zz % 4 % 2, zz % 4 // 2
    row_at = pl.multiple_of(24 * core, 8)
    col_at = pl.multiple_of(384 * chalf, 128)
    gives = parity == shalf

    def own_piece(i):
        ref = (fwd_hbm, back_hbm)[i]
        return pltpu.make_async_copy(
            ref.at[pl.ds(row_at, 24), pl.ds(col_at, 384)],
            mat.at[i, slot, pl.ds(row_at, 24), pl.ds(col_at, 384)], own_sem.at[i],
        )

    @pl.when(gives)
    def _():
        own_piece(0).start()
        own_piece(1).start()

    barrier = pltpu.get_barrier_semaphore()

    def greet(o, carry):
        pl.semaphore_signal(barrier, inc=1, device_id=(ax, (rad + o) % DEV), device_id_type=MESH)
        pl.semaphore_signal(barrier, inc=1, device_id=((ax + o) % DEV, rad), device_id_type=MESH)
        return carry

    lax.fori_loop(1, DEV, greet, 0)

    loads[0].wait()
    loads[1].wait()

    def pack(z, carry):
        esend[0, 0, pl.ds(z, 1), :] = p[z + 1, ROWS - 1 : ROWS, :]
        esend[0, 1, pl.ds(z, 1), :] = 0.5 / h[z + 1, ROWS - 1 : ROWS, :]
        esend[1, 0, pl.ds(z, 1), :] = p[z + 1, 0:1, :]
        esend[1, 1, pl.ds(z, 1), :] = 0.5 / h[z + 1, 0:1, :]
        return carry

    lax.fori_loop(0, ROWS, pack, 0)

    pl.semaphore_wait(barrier, 2 * (DEV - 1))

    def z_halo(side, what):
        edge, slot, to = (ROWS - 1, 0, ax + 1) if side == 0 else (0, ROWS + 1, ax - 1)
        ref, dst = (p_hbm, p) if what == 0 else (d_hbm, h)
        return remote(
            ref.at[edge], dst.at[slot], halo_send.at[side, what], halo_recv.at[side, what], (to, rad)
        )

    def r_halo(side):
        to = rad + 1 if side == 0 else rad - 1
        return remote(
            esend.at[side], ehalo.at[side], halo_send.at[2, side], halo_recv.at[2, side], (ax, to)
        )

    has_above, has_below = ax < DEV - 1, ax > 0
    has_right, has_left = rad < DEV - 1, rad > 0

    @pl.when(has_right)
    def _():
        r_halo(0).start()

    @pl.when(has_left)
    def _():
        r_halo(1).start()

    @pl.when(has_above)
    def _():
        z_halo(0, 0).start()
        z_halo(0, 1).start()

    @pl.when(has_below)
    def _():
        z_halo(1, 0).start()
        z_halo(1, 1).start()

    @pl.when(gives)
    def _():
        for i in range(2):
            own_piece(i).wait()
            piece = mat.at[i, slot, pl.ds(row_at, 24), pl.ds(col_at, 384)]
            for to in peers():
                remote(piece, piece, gat_send.at[i], gat_recv.at[i], (ax, to)).start()

    def weigh(z, carry):
        h[z + 1] = 0.5 / h[z + 1]
        return carry

    lax.fori_loop(0, ROWS, weigh, 0)
    for kh in range(2):
        mu = mu_ref[pl.ds(pl.multiple_of(rad * 2 * KW + kh * KW, 8), KW), :]
        half = 0.5 * (eig_ref[...].reshape(1, MODES) + jnp.concatenate([mu] * TILES, axis=1))
        grow = half + jnp.sqrt(half * (2.0 + half))
        theta = jnp.log1p(grow)
        cst[kh, 0] = theta
        cst[kh, 1] = grow / (1.0 + grow)
        pw[kh, 0] = jnp.ones((KW, MODES), F32)

        def power(j, kappa, kh=kh, theta=theta):
            now = jnp.exp(-(j.astype(F32) * theta))
            kappa = kappa + now * pw[kh, j - 1]
            pw[kh, j] = now
            return kappa

        cst[kh, 2] = lax.fori_loop(1, ROWS + 1, power, jnp.zeros((KW, MODES), F32))

    loads[2].wait()

    @pl.when(has_below)
    def _():
        z_halo(0, 0).wait_recv()
        z_halo(0, 1).wait_recv()
        h[0] = 0.5 / h[0]

    @pl.when(jnp.logical_not(has_below))
    def _():
        p[0] = jnp.zeros((ROWS, AZIM), F32)
        h[0] = jnp.zeros((ROWS, AZIM), F32)

    @pl.when(has_above)
    def _():
        z_halo(1, 0).wait_recv()
        z_halo(1, 1).wait_recv()
        h[ROWS + 1] = 0.5 / h[ROWS + 1]

    @pl.when(jnp.logical_not(has_above))
    def _():
        p[ROWS + 1] = jnp.zeros((ROWS, AZIM), F32)
        h[ROWS + 1] = jnp.zeros((ROWS, AZIM), F32)

    @pl.when(has_left)
    def _():
        r_halo(0).wait_recv()

    @pl.when(jnp.logical_not(has_left))
    def _():
        ehalo[0] = jnp.zeros((2, ROWS, AZIM), F32)

    @pl.when(has_right)
    def _():
        r_halo(1).wait_recv()

    @pl.when(jnp.logical_not(has_right))
    def _():
        ehalo[1] = jnp.zeros((2, ROWS, AZIM), F32)

    def chip(step):
        return ((zz + step) % 8) * 2 + core

    def region(i, step, first, count):
        z4 = (zz + step) % 4
        return mat.at[
            i, pl.ds(z4 // 2 * 8 + first, count), pl.ds(row_at, 24),
            pl.ds(pl.multiple_of(384 * (z4 % 2), 128), 384),
        ]

    def along(i, n):
        step, first, count = ((1, 0, 8), (7, 0, 8), (2, 0, 4), (6, 4, 4))[n]
        part = region(i, 0, first, count)
        return remote(part, part, z_send.at[i, n], z_recv.at[i, n], (chip(step), rad))

    def swap(i, n):
        part = region(i, (0, 7, 1, 2)[n], 0, 8)
        return remote(part, part, c_send.at[i, n], c_recv.at[i, n], (zz * 2 + 1 - core, rad))

    def pass_on(i):
        @pl.when(gives)
        def _():
            await_bytes(mat.at[i, pl.ds(0, 7), pl.ds(0, 24), pl.ds(0, 384)], gat_recv.at[i])

        @pl.when(jnp.logical_not(gives))
        def _():
            await_bytes(mat.at[i, pl.ds(0, 8), pl.ds(0, 24), pl.ds(0, 384)], gat_recv.at[i])

        for n in range(4):
            along(i, n).start()
        swap(i, 0).start()

    def pass_beside(i):
        for n in range(2):
            await_bytes(region(i, 0, 0, 8), z_recv.at[i, n])
            swap(i, 1 + n).start()
        for n in range(2, 4):
            await_bytes(region(i, 0, 0, 4), z_recv.at[i, n])
        swap(i, 3).start()

    def split_mat(i):
        for n in range(4):
            await_bytes(region(i, 0, 0, 8), c_recv.at[i, n])

        def one(t, carry):
            y = t % 8 // 2
            x = t % 2 * 2 + (t // 8 + y) % 2
            at = pl.ds(pl.multiple_of((y * 4 + x) * ROWS, 16), ROWS)
            mh[i, at, :], ml[i, at, :] = split(mat[i, t])
            return carry

        lax.fori_loop(0, DEV, one, 0)

    row = lax.broadcasted_iota(jnp.int32, (ROWS, AZIM), 0)

    def ship_in(kh, c):
        for to in peers():
            remote(
                send.at[c, pl.ds(pl.multiple_of(kh * 128 + to * KW, 8), KW)], recv.at[kh, c, rad],
                f_send.at[kh, c], f_recv.at[kh, c], (ax, to),
            ).start()
        pltpu.make_async_copy(
            send.at[c, pl.ds(pl.multiple_of(kh * 128 + rad * KW, 8), KW)], recv.at[kh, c, rad],
            f_own.at[kh, c],
        ).start()

    def front(c, carry):
        def plane(z):
            mid_p, mid_h = p[z + 1], h[z + 1]
            base = 1.0 - mid_h

            def term(other_p, other_h):
                return (base - other_h) * (other_p - mid_p)

            def radial(side):
                edge = 0 if side == 0 else ROWS - 1
                shift = 1 if side == 0 else ROWS - 1
                return [
                    jnp.where(row == edge, ehalo[side, i, pl.ds(z, 1), :], pltpu.roll(mid, shift, 0))
                    for i, mid in enumerate((mid_p, mid_h))
                ]

            total = src[z] + term(p[z + 2], h[z + 2]) + term(p[z], h[z])
            total = total + term(*radial(1)) + term(*radial(0))
            total = total + term(pltpu.roll(mid_p, 1, 1), pltpu.roll(mid_h, 1, 1))
            return total + term(pltpu.roll(mid_p, AZIM - 1, 1), pltpu.roll(mid_h, AZIM - 1, 1))

        def cells(k, carry):
            parts = [split(plane(c * ZC + 2 * k + q)) for q in range(2)]
            for q, (hi, lo) in enumerate(parts):
                zl = 2 * k + q
                for j in range(3):
                    at = pl.multiple_of((zl // 8) * 384 + j * 128 + (zl % 8) * 16, 16)
                    rh[pl.ds(at, 16), :] = hi[16 * j : 16 * j + 16]
                    rl[pl.ds(at, 16), :] = lo[16 * j : 16 * j + 16]
            return carry

        lax.fori_loop(0, ZC // 2, cells, 0)
        for n in range(3):
            cols = pl.ds(256 * n, 256)
            send[c, :, cols] = dot3(th_ref[...], tl_ref[...], rh[cols, :], rl[cols, :], NT_DIMS)
        ship_in(0, c)

        for i in range(2):
            pl.when(c == i)(functools.partial(pass_on, i))
        return carry

    lax.fori_loop(0, CHUNKS, front, 0)

    def second_half(c, carry):
        ship_in(1, c)
        return carry

    lax.fori_loop(0, CHUNKS, second_half, 0)
    pass_beside(0)

    def regroup_in(kh, c):
        await_bytes(recv.at[0, 0, pl.ds(0, DEV - 1)], f_recv.at[kh, c])
        await_bytes(recv.at[0, 0, 0], f_own.at[kh, c])

        def one(hz, carry):
            groups = []
            for v in range(TILES):
                xs = []
                for e in range(8):
                    s, j = divmod(8 * v + e, 3)
                    xs.append(recv[kh, c, s, :, pl.ds(pl.multiple_of(hz * 384 + j * 128, 128), 128)])
                groups.append(xs)
            groups = [block_transpose(xs, 16) for xs in groups]
            for v, ys in enumerate(groups):
                for i in range(4):
                    at = pl.ds(pl.multiple_of(c * 128 + hz * 64 + i * 16, 16), 16)
                    y = jnp.concatenate(ys[2 * i : 2 * i + 2], axis=0)
                    xh[at, 128 * v : 128 * v + 128], xl[at, 128 * v : 128 * v + 128] = split(y)
            return carry

        lax.fori_loop(0, 2, one, 0)

    def to_owner(kh, t):
        tile = kh * TILES + t
        return remote(
            gsend.at[kh, t], gown.at[ax], r1_send.at[kh, t], r1_recv, (tile + tile // 3, rad)
        )

    def each_owner(kh, act):
        for t in range(TILES):
            tile = kh * TILES + t

            @pl.when(ax != tile + tile // 3)
            def _(t=t):
                act(to_owner(kh, t))

    def upward(kh):
        def transform(n, carry):
            rows = pl.ds(pl.multiple_of(256 * n, 256), 256)
            part = dot3(xh[...], xl[...], mh[0, rows, :], ml[0, rows, :], NT_DIMS)
            spec[kh, :, :, rows] = part.reshape(ROWS, KW, 256)
            return carry

        lax.fori_loop(0, 3, transform, 0)

        def sweep(z, carry):
            g, first = carry
            g = spec[kh, z] + g
            g = g - cst[kh, 1] * g
            spec[kh, z] = g
            return g, first + pw[kh, z] * g

        zero = jnp.zeros((KW, MODES), F32)
        last, first = lax.fori_loop(0, ROWS, sweep, (zero, zero))
        for t, (a, b) in enumerate(zip(tiles_of(last), tiles_of(first))):
            gsend[kh, t, 0] = a
            gsend[kh, t, 1] = b
        each_owner(kh, lambda copy: copy.start())

    tile = jnp.minimum(ax - ax // 4, 2 * TILES - 1)
    my_half, my_tile = tile // TILES, tile % TILES
    is_owner = ax % 4 != 3

    def to_block(kh, o):
        to = (ax + o) % DEV
        return remote(cres.at[to], cin.at[kh, my_tile], r2_send, r2_recv.at[kh], (to, rad))

    def owner(kh):
        @pl.when(is_owner & (my_half == kh))
        def _():
            lanes = pl.ds(pl.multiple_of(128 * my_tile, 128), 128)
            span = pw[kh, ROWS, :, lanes]
            kap = cst[kh, 2, :, lanes]
            th = cst[kh, 0, :, lanes]
            await_bytes(gown.at[pl.ds(0, DEV - 1)], r1_recv)
            gown[ax] = gsend[kh, my_tile]
            enter = jnp.zeros((8, 128), F32)
            for a in range(DEV):
                cres[a, 0] = enter
                enter = gown[a, 0] + span * enter
            enter = jnp.zeros((8, 128), F32)
            for a in range(DEV - 1, -1, -1):
                cres[a, 1] = enter
                enter = gown[a, 1] + kap * cres[a, 0] + span * enter
            ghost = enter * jnp.exp(-th) / (1.0 - jnp.exp(-float(2 * MODES + 2) * th))
            for a in range(DEV):
                cres[a, 2] = ghost

            def back(o, carry):
                to_block(kh, o).start()
                return carry

            lax.fori_loop(1, DEV, back, 0)
            cin[kh, my_tile] = cres[ax]

    def enter(kh):
        @pl.when(is_owner & (my_half == kh))
        def _():
            await_bytes(cin.at[kh, pl.ds(0, TILES - 1)], r2_recv.at[kh])

        @pl.when(jnp.logical_not(is_owner & (my_half == kh)))
        def _():
            await_bytes(cin.at[kh], r2_recv.at[kh])

        below, above, ghost = [
            jnp.concatenate([cin[kh, t, i] for t in range(TILES)], axis=1) for i in range(3)
        ]
        start = (ax * ROWS).astype(F32)
        cst[kh, 3] = below
        cst[kh, 4] = ghost * jnp.exp(-start * cst[kh, 0])
        cst[kh, 5] = ghost * jnp.exp(-(float(2 * MODES + 1 - ROWS) - start) * cst[kh, 0])

        state[kh] = above

    def lower(kh, c):
        def sweep(k, u):
            pair = ZC // 2 - 1 - k
            res = [None, None]
            for q in (1, 0):
                z = c * ZC + 2 * pair + q
                up, down = pw[kh, z + 1], pw[kh, ROWS - z]
                u = (spec[kh, z] + up * cst[kh, 3]) + (u - cst[kh, 1] * u)
                res[q] = u - cst[kh, 4] * up + cst[kh, 5] * down
            hi, lo = split(jnp.concatenate(res, axis=0))
            at = pl.multiple_of(pair * 2 * KW, 16)
            uu[pl.ds(at, 2 * KW), :] = hi
            uu[pl.ds(ZC * KW + at, 2 * KW), :] = lo
            return u

        state[kh] = lax.fori_loop(0, ZC // 2, sweep, state[kh])

        def transform(n, carry):
            rows = pl.ds(pl.multiple_of(256 * n, 256), 256)
            both = lax.dot_general(mh[1, rows, :], uu[...], NT_DIMS, preferred_element_type=F32)
            low = lax.dot_general(
                ml[1, rows, :], uu[: ZC * KW, :], NT_DIMS, preferred_element_type=F32
            )
            bsend[kh, c, rows, :] = both[:, : ZC * KW] + (both[:, ZC * KW :] + low)
            return carry

        lax.fori_loop(0, 3, transform, 0)
        for to in peers():
            remote(
                bsend.at[kh, c, pl.ds(pl.multiple_of(to * ROWS, 8), ROWS)], brecv.at[kh, c, rad],
                b_send.at[kh, c], b_recv.at[kh, c], (ax, to),
            ).start()
        pltpu.make_async_copy(
            bsend.at[kh, c, pl.ds(pl.multiple_of(rad * ROWS, 8), ROWS)], brecv.at[kh, c, rad],
            b_own.at[kh, c],
        ).start()

    def lower_rest(kh, count):
        def one(i, carry):
            lower(kh, count - 1 - i)
            return carry

        lax.fori_loop(0, count, one, 0)

    split_mat(0)
    for c in range(CHUNKS):
        regroup_in(0, c)
    upward(0)
    regroup_in(1, 0)
    owner(0)
    pass_beside(1)
    regroup_in(1, 1)
    split_mat(1)
    enter(0)
    lower(0, CHUNKS - 1)
    regroup_in(1, 2)
    upward(1)
    lower_rest(0, CHUNKS - 1)
    owner(1)
    enter(1)
    lower_rest(1, CHUNKS)

    def regroup_out(kh, c):
        await_bytes(brecv.at[0, 0, pl.ds(0, DEV - 1)], b_recv.at[kh, c])
        await_bytes(brecv.at[0, 0, 0], b_own.at[kh, c])

        def one(rt, carry):
            xs = [brecv[kh, c, d, pl.ds(pl.multiple_of(rt * 16, 8), 16), :] for d in range(DEV)]
            for zl, y in enumerate(block_transpose(xs, 8)):
                at = pl.ds(pl.multiple_of(c * UNIT + zl * ROWS + rt * 16, 16), 16)
                yh[at, 128 * kh : 128 * kh + 128], yl[at, 128 * kh : 128 * kh + 128] = split(y)
            return carry

        lax.fori_loop(0, 3, one, 0)

    def early(i, carry):
        regroup_out(0, CHUNKS - 1 - i)
        return carry

    lax.fori_loop(0, CHUNKS, early, 0)

    def finish(i, carry):
        c = CHUNKS - 1 - i
        regroup_out(1, c)

        def transform(n, carry):
            rows = pl.ds(pl.multiple_of(c * UNIT + 256 * n, 256), 256)
            part = dot3(yh[rows, :], yl[rows, :], th_ref[...], tl_ref[...], NN_DIMS)
            out[rows, :] = part * (1.0 / AZIM)
            return carry

        lax.fori_loop(0, 3, transform, 0)
        at = pl.ds(pl.multiple_of(c * UNIT, 256), UNIT)
        pltpu.make_async_copy(out.at[at], out_hbm.at[at], out_sem.at[c]).start()
        return carry

    lax.fori_loop(0, CHUNKS, finish, 0)

    @pl.when(has_above)
    def _():
        z_halo(0, 0).wait_send()
        z_halo(0, 1).wait_send()

    @pl.when(has_below)
    def _():
        z_halo(1, 0).wait_send()
        z_halo(1, 1).wait_send()

    @pl.when(has_right)
    def _():
        r_halo(0).wait_send()

    @pl.when(has_left)
    def _():
        r_halo(1).wait_send()

    @pl.when(gives)
    def _():
        for i in range(2):
            await_bytes(mat.at[i, pl.ds(0, DEV - 1), pl.ds(0, 24), pl.ds(0, 384)], gat_send.at[i])

    for i in range(2):
        for n in range(4):
            along(i, n).wait_send()
            swap(i, n).wait_send()
    for kh in range(2):
        each_owner(kh, lambda copy: copy.wait_send())

    @pl.when(is_owner)
    def _():
        await_bytes(cres.at[pl.ds(0, DEV - 1)], r2_send)

    def drain(c, carry):
        for kh in range(2):
            await_bytes(recv.at[0, 0, pl.ds(0, DEV - 1)], f_send.at[kh, c])
            await_bytes(brecv.at[0, 0, pl.ds(0, DEV - 1)], b_send.at[kh, c])
        at = pl.ds(pl.multiple_of(c * UNIT, 256), UNIT)
        pltpu.make_async_copy(out.at[at], out_hbm.at[at], out_sem.at[c]).wait()
        return carry

    lax.fori_loop(0, CHUNKS, drain, 0)


def constants():
    index = np.arange(AZIM)
    angle = 2.0 * np.pi * (index[:, None] * index[None, :] % AZIM) / AZIM
    table = (np.cos(angle) + np.sin(angle)).astype(np.float32)
    hi = table.astype(jnp.bfloat16)
    lo = (table - hi.astype(np.float32)).astype(jnp.bfloat16)
    order = np.arange(AZIM).reshape(DEV, 2, KW).transpose(1, 0, 2).reshape(-1)
    hi, lo = hi[order], lo[order]
    mu = (2.0 - 2.0 * np.cos(2.0 * np.pi * index / AZIM)).astype(np.float32)
    return hi, lo, np.ascontiguousarray(np.broadcast_to(mu[:, None], (AZIM, 128)))


def body(source, pressure_old, density, radial_forward, radial_back, radial_eig):
    hi, lo, mu = constants()
    anywhere = pl.BlockSpec(memory_space=pl.ANY)
    vmem = pl.BlockSpec(memory_space=pltpu.VMEM)
    dma = pltpu.SemaphoreType.DMA
    result = pl.pallas_call(
        kernel,
        out_shape=jax.ShapeDtypeStruct((ROWS * ROWS, AZIM), F32),
        in_specs=[anywhere] * 5 + [vmem] * 4,
        out_specs=anywhere,
        scratch_shapes=[
            pltpu.VMEM((ROWS, ROWS, AZIM), F32),
            pltpu.VMEM((ROWS + 2, ROWS, AZIM), F32),
            pltpu.VMEM((ROWS + 2, ROWS, AZIM), F32),
            pltpu.VMEM((2, 2, ROWS, AZIM), F32),
            pltpu.VMEM((2, 2, ROWS, AZIM), F32),
            pltpu.VMEM((UNIT, AZIM), BF16),
            pltpu.VMEM((UNIT, AZIM), BF16),
            pltpu.VMEM((CHUNKS, AZIM, UNIT), F32),
            pltpu.VMEM((2, CHUNKS, DEV, KW, UNIT), F32),
            pltpu.VMEM((ROWS * KW, MODES), BF16),
            pltpu.VMEM((ROWS * KW, MODES), BF16),
            pltpu.VMEM((2, ROWS, KW, MODES), F32),
            pltpu.VMEM((2, ROWS + 1, KW, MODES), F32),
            pltpu.VMEM((2, DEV, ROWS, MODES), F32),
            pltpu.VMEM((2, MODES, MODES), BF16),
            pltpu.VMEM((2, MODES, MODES), BF16),
            pltpu.VMEM((2 * ZC * KW, MODES), BF16),
            pltpu.VMEM((2, CHUNKS, MODES, ZC * KW), F32),
            pltpu.VMEM((2, CHUNKS, DEV, ROWS, ZC * KW), F32),
            pltpu.VMEM((ROWS * ROWS, AZIM), BF16),
            pltpu.VMEM((ROWS * ROWS, AZIM), BF16),
            pltpu.VMEM((ROWS * ROWS, AZIM), F32),
            pltpu.VMEM((2, 6, KW, MODES), F32),
            pltpu.VMEM((2, KW, MODES), F32),
            pltpu.VMEM((2, TILES, 2, 8, 128), F32),
            pltpu.VMEM((DEV, 2, 8, 128), F32),
            pltpu.VMEM((DEV, 3, 8, 128), F32),
            pltpu.VMEM((2, TILES, 3, 8, 128), F32),
            dma((3,)), dma((2,)), dma((3, 2)), dma((3, 2)), dma((2,)), dma((2,)), dma((2, 4)),
            dma((2, 4)), dma((2, 4)), dma((2, 4)), dma((2, CHUNKS)), dma((2, CHUNKS)), dma((2, CHUNKS)),
            dma((2, CHUNKS)), dma((2, CHUNKS)), dma((2, CHUNKS)), dma((2, TILES)), dma, dma,
            dma((2,)), dma((CHUNKS,)),
        ],
        compiler_params=pltpu.CompilerParams(
            collective_id=0, has_side_effects=True, vmem_limit_bytes=60 * 1024 * 1024
        ),
    )(
        source, pressure_old, density, radial_forward, radial_back,
        radial_eig, jnp.asarray(mu), jnp.asarray(hi), jnp.asarray(lo),
    )
    return result.reshape(ROWS, ROWS, AZIM)


def solution(mesh):
    in_specs = (
        P("axial", "radial", None),
        P("axial", "radial", None),
        P("axial", "radial", None),
        P("radial", None),
        P("radial", None),
        P(),
    )
    out_specs = P("axial", "radial", None)
    return jax.shard_map(body, mesh=mesh, in_specs=in_specs, out_specs=out_specs, check_vma=False)
```

```python
import functools

import jax
import jax.numpy as jnp
import numpy as np
from jax import lax
from jax.experimental import pallas as pl
from jax.experimental.pallas import tpu as pltpu
from jax.sharding import PartitionSpec as P

MESH = pl.DeviceIdType.MESH
F32, BF16 = jnp.float32, jnp.bfloat16
DEV = 16
ROWS = 48
AZIM = 256
MODES = 768
KW = 8
ZC = 16
CHUNKS = ROWS // ZC
TILES = 6
LANES = MODES // 2
UNIT = ZC * ROWS
OFFSETS = (
    (0, 1), (0, 3), (1, 0), (3, 0), (1, 1), (3, 3), (1, 3), (3, 1), (0, 2), (2, 0), (2, 2), (1, 2), (3, 2), (2, 1), (2, 3),
)
NT_DIMS = (((1,), (1,)), ((), ()))
NN_DIMS = (((1,), (0,)), ((), ()))


def split(x):
    hi = x.astype(BF16)
    return hi, (x - hi.astype(F32)).astype(BF16)


def dot3(ah, al, bh, bl, dims):
    def dot(a, b):
        return lax.dot_general(a, b, dims, preferred_element_type=F32)

    return dot(ah, bh) + (dot(ah, bl) + dot(al, bh))


def block_transpose(xs, width):
    lane = lax.broadcasted_iota(jnp.int32, xs[0].shape, 1)
    xs = list(xs)
    step = len(xs) // 2
    while step:
        shift = width * step
        low = (lane & shift) == 0
        for i in range(len(xs)):
            if i & step:
                continue
            a, b = xs[i], xs[i + step]
            if shift == 64:
                moved = pltpu.roll(jnp.where(low, b, a), 64, 1)
                xs[i], xs[i + step] = jnp.where(low, a, moved), jnp.where(low, moved, b)
            else:
                xs[i] = jnp.where(low, a, pltpu.roll(b, shift, 1))
                xs[i + step] = jnp.where(low, pltpu.roll(a, 128 - shift, 1), b)
        step //= 2
    return xs


def kernel(
    src_hbm, p_hbm, d_hbm, fwd_hbm, back_hbm, eig_ref, mu_ref, table_ref, out_hbm,
    th_ref, tl_ref, src, p, h, esend, ehalo, rh, rl, send, recv, xh, xl, spec, pw, mat, mh, ml, uu,
    bsend, brecv, yh, yl, out, cst, state, gsend, gpair, gchip, entry, csend, cin,
    load_sem, own_sem, halo_send, halo_recv, gat_send, gat_recv, z_send, z_recv, c_send, c_recv,
    f_send, f_recv, f_own, b_send, b_recv, b_own, x1_send, x1_recv, x2_send, x2_recv, x3_send, x3_recv, out_sem,
):
    ax, rad = lax.axis_index("axial"), lax.axis_index("radial")
    zz, core = ax // 2, ax % 2
    ry, rx = rad // 4, rad % 4

    def remote(src_ref, dst_ref, send_sem, recv_sem, device):
        return pltpu.make_async_remote_copy(
            src_ref=src_ref, dst_ref=dst_ref, send_sem=send_sem, recv_sem=recv_sem,
            device_id=device, device_id_type=MESH,
        )

    def await_bytes(ref, sem):
        pltpu.make_async_copy(ref, ref, sem).wait()

    def peers():
        for a, b in OFFSETS:
            yield ((ry + a + core * (b - a)) % 4) * 4 + (rx + b + core * (a - b)) % 4

    loads = [
        pltpu.make_async_copy(p_hbm, p.at[pl.ds(1, ROWS)], load_sem.at[0]),
        pltpu.make_async_copy(d_hbm, h.at[pl.ds(1, ROWS)], load_sem.at[1]),
        pltpu.make_async_copy(src_hbm, src, load_sem.at[2]),
    ]
    for load in loads:
        load.start()
    parity = (ry + rx) % 2
    slot = parity * 8 + ry * 2 + rx // 2
    chalf, shalf = zz % 4 % 2, zz % 4 // 2
    row_at = pl.multiple_of(24 * core, 8)
    col_at = pl.multiple_of(384 * chalf, 128)
    gives = (parity == shalf, parity != shalf)

    def own_piece(i):
        ref = (fwd_hbm, back_hbm)[i]
        return pltpu.make_async_copy(
            ref.at[pl.ds(row_at, 24), pl.ds(col_at, 384)],
            mat.at[i, slot, pl.ds(row_at, 24), pl.ds(col_at, 384)], own_sem.at[i],
        )

    for i in range(2):
        pl.when(gives[i])(lambda i=i: own_piece(i).start())

    barrier = pltpu.get_barrier_semaphore()

    def greet(o, carry):
        pl.semaphore_signal(barrier, inc=1, device_id=(ax, (rad + o) % DEV), device_id_type=MESH)
        pl.semaphore_signal(barrier, inc=1, device_id=((ax + o) % DEV, rad), device_id_type=MESH)
        return carry

    lax.fori_loop(1, DEV, greet, 0)

    loads[0].wait()
    loads[1].wait()

    def pack(z, carry):
        esend[0, 0, pl.ds(z, 1), :] = p[z + 1, ROWS - 1 : ROWS, :]
        esend[0, 1, pl.ds(z, 1), :] = 0.5 / h[z + 1, ROWS - 1 : ROWS, :]
        esend[1, 0, pl.ds(z, 1), :] = p[z + 1, 0:1, :]
        esend[1, 1, pl.ds(z, 1), :] = 0.5 / h[z + 1, 0:1, :]
        return carry

    lax.fori_loop(0, ROWS, pack, 0)

    pl.semaphore_wait(barrier, 2 * (DEV - 1))

    def z_halo(side, what):
        edge, slot, to = (ROWS - 1, 0, ax + 1) if side == 0 else (0, ROWS + 1, ax - 1)
        ref, dst = (p_hbm, p) if what == 0 else (d_hbm, h)
        return remote(
            ref.at[edge], dst.at[slot], halo_send.at[side, what], halo_recv.at[side, what], (to, rad)
        )

    def r_halo(side):
        to = rad + 1 if side == 0 else rad - 1
        return remote(
            esend.at[side], ehalo.at[side], halo_send.at[2, side], halo_recv.at[2, side], (ax, to)
        )

    has_above, has_below = ax < DEV - 1, ax > 0
    has_right, has_left = rad < DEV - 1, rad > 0

    @pl.when(has_right)
    def _():
        r_halo(0).start()

    @pl.when(has_left)
    def _():
        r_halo(1).start()

    @pl.when(has_above)
    def _():
        z_halo(0, 0).start()
        z_halo(0, 1).start()

    @pl.when(has_below)
    def _():
        z_halo(1, 0).start()
        z_halo(1, 1).start()

    def offer(i):
        @pl.when(gives[i])
        def _():
            own_piece(i).wait()
            piece = mat.at[i, slot, pl.ds(row_at, 24), pl.ds(col_at, 384)]
            for to in peers():
                remote(piece, piece, gat_send.at[i], gat_recv.at[i], (ax, to)).start()

    offer(0)
    offer(1)

    def weigh(z, carry):
        h[z + 1] = 0.5 / h[z + 1]
        return carry

    lax.fori_loop(0, ROWS, weigh, 0)
    for kh in range(2):
        mu = mu_ref[pl.ds(pl.multiple_of(rad * 2 * KW + kh * KW, 8), KW), :]
        half = 0.5 * (eig_ref[...].reshape(1, MODES) + jnp.concatenate([mu] * TILES, axis=1))
        grow = half + jnp.sqrt(half * (2.0 + half))
        theta = jnp.log1p(grow)
        cst[kh, 0] = theta
        cst[kh, 1] = grow / (1.0 + grow)
        pw[kh, 0] = jnp.ones((KW, MODES), F32)

        def power(j, kappa, kh=kh, theta=theta):
            now = jnp.exp(-(j.astype(F32) * theta))
            kappa = kappa + now * pw[kh, j - 1]
            pw[kh, j] = now
            return kappa

        cst[kh, 2] = lax.fori_loop(1, ROWS + 1, power, jnp.zeros((KW, MODES), F32))

    th_ref[...], tl_ref[...] = split(table_ref[...])
    loads[2].wait()

    @pl.when(has_below)
    def _():
        z_halo(0, 0).wait_recv()
        z_halo(0, 1).wait_recv()
        h[0] = 0.5 / h[0]

    @pl.when(jnp.logical_not(has_below))
    def _():
        p[0] = jnp.zeros((ROWS, AZIM), F32)
        h[0] = jnp.zeros((ROWS, AZIM), F32)

    @pl.when(has_above)
    def _():
        z_halo(1, 0).wait_recv()
        z_halo(1, 1).wait_recv()
        h[ROWS + 1] = 0.5 / h[ROWS + 1]

    @pl.when(jnp.logical_not(has_above))
    def _():
        p[ROWS + 1] = jnp.zeros((ROWS, AZIM), F32)
        h[ROWS + 1] = jnp.zeros((ROWS, AZIM), F32)

    @pl.when(has_left)
    def _():
        r_halo(0).wait_recv()

    @pl.when(jnp.logical_not(has_left))
    def _():
        ehalo[0] = jnp.zeros((2, ROWS, AZIM), F32)

    @pl.when(has_right)
    def _():
        r_halo(1).wait_recv()

    @pl.when(jnp.logical_not(has_right))
    def _():
        ehalo[1] = jnp.zeros((2, ROWS, AZIM), F32)

    def chip(step):
        return ((zz + step) % 8) * 2 + core

    def region(i, step, first, count):
        z4 = (zz + step) % 4
        return mat.at[
            i, pl.ds((z4 // 2 + i) % 2 * 8 + first, count), pl.ds(row_at, 24),
            pl.ds(pl.multiple_of(384 * (z4 % 2), 128), 384),
        ]

    def along(i, n):
        up, of, first, count = ((1, 0, 0, 8), (7, 0, 0, 8), (1, 7, 0, 4), (7, 1, 4, 4))[n]
        part = region(i, of, first, count)
        return remote(part, part, z_send.at[i, n], z_recv.at[i, n], (chip(up), rad))

    def swap(i, n):
        part = region(i, (0, 7, 1, 2)[n], 0, 8)
        return remote(part, part, c_send.at[i, n], c_recv.at[i, n], (zz * 2 + 1 - core, rad))

    def pass_on(i):
        @pl.when(gives[i])
        def _():
            await_bytes(mat.at[i, pl.ds(0, 7), pl.ds(0, 24), pl.ds(0, 384)], gat_recv.at[i])

        @pl.when(jnp.logical_not(gives[i]))
        def _():
            await_bytes(mat.at[i, pl.ds(0, 8), pl.ds(0, 24), pl.ds(0, 384)], gat_recv.at[i])

        for n in range(2):
            along(i, n).start()
        swap(i, 0).start()

    def pass_further(i):
        for n in range(2):
            await_bytes(region(i, 0, 0, 8), z_recv.at[i, n])
            along(i, 2 + n).start()
            swap(i, 1 + n).start()

    def pass_last(i):
        for n in range(2, 4):
            await_bytes(region(i, 0, 0, 4), z_recv.at[i, n])
        swap(i, 3).start()

    def split_mat(i):
        for n in range(4):
            await_bytes(region(i, 0, 0, 8), c_recv.at[i, n])

        def one(t, carry):
            y = t % 8 // 2
            x = t % 2 * 2 + (t // 8 + y) % 2
            at = pl.ds(pl.multiple_of((y * 4 + x) * ROWS, 16), ROWS)
            mh[i, at, :], ml[i, at, :] = split(mat[i, t])
            return carry

        lax.fori_loop(0, DEV, one, 0)

    row = lax.broadcasted_iota(jnp.int32, (ROWS, AZIM), 0)

    def ship_in(kh, c):
        for to in peers():
            remote(
                send.at[c, pl.ds(pl.multiple_of(kh * 128 + to * KW, 8), KW)], recv.at[kh, c, rad],
                f_send.at[kh, c], f_recv.at[kh, c], (ax, to),
            ).start()
        pltpu.make_async_copy(
            send.at[c, pl.ds(pl.multiple_of(kh * 128 + rad * KW, 8), KW)], recv.at[kh, c, rad],
            f_own.at[kh, c],
        ).start()

    def front(c, carry):
        def plane(z):
            mid_p, mid_h = p[z + 1], h[z + 1]
            base = 1.0 - mid_h

            def term(other_p, other_h):
                return (base - other_h) * (other_p - mid_p)

            def radial(side):
                edge = 0 if side == 0 else ROWS - 1
                shift = 1 if side == 0 else ROWS - 1
                return [
                    jnp.where(row == edge, ehalo[side, i, pl.ds(z, 1), :], pltpu.roll(mid, shift, 0))
                    for i, mid in enumerate((mid_p, mid_h))
                ]

            total = src[z] + term(p[z + 2], h[z + 2]) + term(p[z], h[z])
            total = total + term(*radial(1)) + term(*radial(0))
            total = total + term(pltpu.roll(mid_p, 1, 1), pltpu.roll(mid_h, 1, 1))
            return total + term(pltpu.roll(mid_p, AZIM - 1, 1), pltpu.roll(mid_h, AZIM - 1, 1))

        def cells(k, carry):
            parts = [split(plane(c * ZC + 2 * k + q)) for q in range(2)]
            for q, (hi, lo) in enumerate(parts):
                zl = 2 * k + q
                for j in range(3):
                    at = pl.multiple_of((zl // 8) * 384 + j * 128 + (zl % 8) * 16, 16)
                    rh[pl.ds(at, 16), :] = hi[16 * j : 16 * j + 16]
                    rl[pl.ds(at, 16), :] = lo[16 * j : 16 * j + 16]
            return carry

        lax.fori_loop(0, ZC // 2, cells, 0)
        for n in range(3):
            cols = pl.ds(256 * n, 256)
            send[c, :, cols] = dot3(th_ref[...], tl_ref[...], rh[cols, :], rl[cols, :], NT_DIMS)
        ship_in(0, c)

        for i in range(2):
            pl.when(c == i)(functools.partial(pass_on, i))
        return carry

    lax.fori_loop(0, CHUNKS, front, 0)

    def second_half(c, carry):
        ship_in(1, c)
        return carry

    lax.fori_loop(0, CHUNKS, second_half, 0)
    pass_further(0)

    def regroup_in(kh, c):
        await_bytes(recv.at[0, 0, pl.ds(0, DEV - 1)], f_recv.at[kh, c])
        await_bytes(recv.at[0, 0, 0], f_own.at[kh, c])

        def one(hz, carry):
            groups = []
            for v in range(TILES):
                xs = []
                for e in range(8):
                    s, j = divmod(8 * v + e, 3)
                    xs.append(recv[kh, c, s, :, pl.ds(pl.multiple_of(hz * 384 + j * 128, 128), 128)])
                groups.append(xs)
            groups = [block_transpose(xs, 16) for xs in groups]
            for v, ys in enumerate(groups):
                for i in range(4):
                    at = pl.ds(pl.multiple_of(c * 128 + hz * 64 + i * 16, 16), 16)
                    y = jnp.concatenate(ys[2 * i : 2 * i + 2], axis=0)
                    xh[at, 128 * v : 128 * v + 128], xl[at, 128 * v : 128 * v + 128] = split(y)
            return carry

        lax.fori_loop(0, 2, one, 0)

    def half_lanes(which):
        return pl.ds(pl.multiple_of(which * LANES, 128), LANES)

    beside = (zz * 2 + 1 - core, rad)

    def to_beside(kh):
        return remote(
            gsend.at[kh, :, :, half_lanes(1 - core)], gpair.at[kh], x1_send.at[kh], x1_recv.at[kh], beside
        )

    def to_chips(kh, step):
        own = gchip.at[kh, zz]
        return remote(own, own, x2_send.at[kh], x2_recv.at[kh], (chip(step), rad))

    def answer(kh):
        return remote(
            csend.at[kh], cin.at[kh, :, :, half_lanes(core)], x3_send.at[kh], x3_recv.at[kh], beside
        )

    def both_blocks(kh):
        mine = [gsend[kh, i, :, half_lanes(core)] for i in range(2)]
        theirs = [gpair[kh, i] for i in range(2)]
        low = [jnp.where(core == 0, a, b) for a, b in zip(mine, theirs)]
        high = [jnp.where(core == 0, b, a) for a, b in zip(mine, theirs)]
        span, kappa = pw[kh, ROWS, :, half_lanes(core)], cst[kh, 2, :, half_lanes(core)]
        return low, high, span, kappa

    def join(kh):
        to_beside(kh).wait_recv()
        (low_g, low_u), (high_g, high_u), span, kappa = both_blocks(kh)
        gchip[kh, zz, 0] = high_g + span * low_g
        gchip[kh, zz, 1] = low_u + span * (high_u + kappa * low_g)

        def one(step, carry):
            to_chips(kh, step).start()
            return carry

        lax.fori_loop(1, 8, one, 0)

    def resolve(kh):
        await_bytes(gchip.at[kh, pl.ds(0, 7)], x2_recv.at[kh])
        (low_g, low_u), (high_g, high_u), span, kappa = both_blocks(kh)
        wide, kappa2 = span * span, kappa * (1.0 + span * span)
        enter = jnp.zeros((KW, LANES), F32)
        for z in range(8):
            entry[0, z] = enter
            enter = gchip[kh, z, 0] + wide * enter
        enter = jnp.zeros((KW, LANES), F32)
        for z in range(7, -1, -1):
            entry[1, z] = enter
            enter = gchip[kh, z, 1] + kappa2 * entry[0, z] + wide * enter
        th = cst[kh, 0, :, half_lanes(core)]
        ghost = enter * jnp.exp(-th) / (1.0 - jnp.exp(-float(2 * MODES + 2) * th))
        low_in, high_up = entry[0, zz], entry[1, zz]
        high_in = low_g + span * low_in
        low_up = high_u + kappa * high_in + span * high_up
        for i, (a, b) in enumerate(((low_in, high_in), (low_up, high_up), (ghost, ghost))):
            cin[kh, i, :, half_lanes(core)] = jnp.where(core == 0, a, b)
            csend[kh, i] = jnp.where(core == 0, b, a)
        answer(kh).start()

    def upward(kh, c, count):
        cells = pl.ds(c * ZC, count * ZC)
        part_rows = pl.ds(c * ZC * KW, count * ZC * KW)

        def transform(n, carry):
            rows = pl.ds(pl.multiple_of(256 * n, 256), 256)
            part = dot3(xh[part_rows, :], xl[part_rows, :], mh[0, rows, :], ml[0, rows, :], NT_DIMS)
            spec[kh, cells, :, rows] = part.reshape(count * ZC, KW, 256)
            return carry

        lax.fori_loop(0, 3, transform, 0)

        def sweep(z, carry):
            g, first = carry
            g = spec[kh, z] + g
            g = g - cst[kh, 1] * g
            spec[kh, z] = g
            return g, first + pw[kh, z] * g

        zero = jnp.zeros((KW, MODES), F32)
        begin = (zero, zero) if c == 0 else (gsend[kh, 0], gsend[kh, 1])
        last, first = lax.fori_loop(c * ZC, (c + count) * ZC, sweep, begin)
        gsend[kh, 0] = last
        gsend[kh, 1] = first

    def exchange(kh):
        to_beside(kh).start()
        join(kh)

    def enter(kh):
        answer(kh).wait_recv()
        below, above, ghost = cin[kh, 0], cin[kh, 1], cin[kh, 2]
        start = (ax * ROWS).astype(F32)
        cst[kh, 3] = below
        cst[kh, 4] = ghost * jnp.exp(-start * cst[kh, 0])
        cst[kh, 5] = ghost * jnp.exp(-(float(2 * MODES + 1 - ROWS) - start) * cst[kh, 0])

        state[kh] = above

    def lower(kh, c):
        def sweep(k, u):
            pair = ZC // 2 - 1 - k
            res = [None, None]
            for q in (1, 0):
                z = c * ZC + 2 * pair + q
                up, down = pw[kh, z + 1], pw[kh, ROWS - z]
                u = (spec[kh, z] + up * cst[kh, 3]) + (u - cst[kh, 1] * u)
                res[q] = u - cst[kh, 4] * up + cst[kh, 5] * down
            hi, lo = split(jnp.concatenate(res, axis=0))
            at = pl.multiple_of(pair * 2 * KW, 16)
            uu[pl.ds(at, 2 * KW), :] = hi
            uu[pl.ds(ZC * KW + at, 2 * KW), :] = lo
            return u

        state[kh] = lax.fori_loop(0, ZC // 2, sweep, state[kh])

        def transform(n, carry):
            rows = pl.ds(pl.multiple_of(256 * n, 256), 256)
            both = lax.dot_general(mh[1, rows, :], uu[...], NT_DIMS, preferred_element_type=F32)
            low = lax.dot_general(
                ml[1, rows, :], uu[: ZC * KW, :], NT_DIMS, preferred_element_type=F32
            )
            bsend[kh, c, rows, :] = both[:, : ZC * KW] + (both[:, ZC * KW :] + low)
            return carry

        lax.fori_loop(0, 3, transform, 0)
        for to in peers():
            remote(
                bsend.at[kh, c, pl.ds(pl.multiple_of(to * ROWS, 8), ROWS)], brecv.at[kh, c, rad],
                b_send.at[kh, c], b_recv.at[kh, c], (ax, to),
            ).start()
        pltpu.make_async_copy(
            bsend.at[kh, c, pl.ds(pl.multiple_of(rad * ROWS, 8), ROWS)], brecv.at[kh, c, rad],
            b_own.at[kh, c],
        ).start()

    def lower_rest(kh, count):
        def one(i, carry):
            lower(kh, count - 1 - i)
            return carry

        lax.fori_loop(0, count, one, 0)

    regroup_in(0, 0)
    regroup_in(0, 1)
    pass_last(0)
    regroup_in(0, 2)
    split_mat(0)
    pass_further(1)
    upward(0, 0, CHUNKS)
    exchange(0)
    regroup_in(1, 0)
    pass_last(1)
    regroup_in(1, 1)
    upward(1, 0, 2)
    resolve(0)
    split_mat(1)
    enter(0)
    lower(0, CHUNKS - 1)
    regroup_in(1, 2)
    upward(1, 2, 1)
    exchange(1)
    lower_rest(0, CHUNKS - 1)
    resolve(1)
    enter(1)
    lower_rest(1, CHUNKS)

    def regroup_out(kh, c):
        await_bytes(brecv.at[0, 0, pl.ds(0, DEV - 1)], b_recv.at[kh, c])
        await_bytes(brecv.at[0, 0, 0], b_own.at[kh, c])

        def one(rt, carry):
            xs = [brecv[kh, c, d, pl.ds(pl.multiple_of(rt * 16, 8), 16), :] for d in range(DEV)]
            for zl, y in enumerate(block_transpose(xs, 8)):
                at = pl.ds(pl.multiple_of(c * UNIT + zl * ROWS + rt * 16, 16), 16)
                yh[at, 128 * kh : 128 * kh + 128], yl[at, 128 * kh : 128 * kh + 128] = split(y)
            return carry

        lax.fori_loop(0, 3, one, 0)

    def early(i, carry):
        regroup_out(0, CHUNKS - 1 - i)
        return carry

    lax.fori_loop(0, CHUNKS, early, 0)

    def finish(i, carry):
        c = CHUNKS - 1 - i
        regroup_out(1, c)

        def transform(n, carry):
            rows = pl.ds(pl.multiple_of(c * UNIT + 256 * n, 256), 256)
            part = dot3(yh[rows, :], yl[rows, :], th_ref[...], tl_ref[...], NN_DIMS)
            out[rows, :] = part * (1.0 / AZIM)
            return carry

        lax.fori_loop(0, 3, transform, 0)
        at = pl.ds(pl.multiple_of(c * UNIT, 256), UNIT)
        pltpu.make_async_copy(out.at[at], out_hbm.at[at], out_sem.at[c]).start()
        return carry

    lax.fori_loop(0, CHUNKS, finish, 0)

    @pl.when(has_above)
    def _():
        z_halo(0, 0).wait_send()
        z_halo(0, 1).wait_send()

    @pl.when(has_below)
    def _():
        z_halo(1, 0).wait_send()
        z_halo(1, 1).wait_send()

    @pl.when(has_right)
    def _():
        r_halo(0).wait_send()

    @pl.when(has_left)
    def _():
        r_halo(1).wait_send()

    for i in range(2):

        @pl.when(gives[i])
        def _(i=i):
            await_bytes(mat.at[i, pl.ds(0, DEV - 1), pl.ds(0, 24), pl.ds(0, 384)], gat_send.at[i])

    for i in range(2):
        for n in range(4):
            along(i, n).wait_send()
            swap(i, n).wait_send()
    for kh in range(2):
        to_beside(kh).wait_send()
        await_bytes(gchip.at[kh, pl.ds(0, 7)], x2_send.at[kh])
        answer(kh).wait_send()

    def drain(c, carry):
        for kh in range(2):
            await_bytes(recv.at[0, 0, pl.ds(0, DEV - 1)], f_send.at[kh, c])
            await_bytes(brecv.at[0, 0, pl.ds(0, DEV - 1)], b_send.at[kh, c])
        at = pl.ds(pl.multiple_of(c * UNIT, 256), UNIT)
        pltpu.make_async_copy(out.at[at], out_hbm.at[at], out_sem.at[c]).wait()
        return carry

    lax.fori_loop(0, CHUNKS, drain, 0)


def constants():
    index = np.arange(AZIM)
    angle = 2.0 * np.pi * (index[:, None] * index[None, :] % AZIM) / AZIM
    table = (np.cos(angle) + np.sin(angle)).astype(np.float32)
    order = np.arange(AZIM).reshape(DEV, 2, KW).transpose(1, 0, 2).reshape(-1)
    mu = (2.0 - 2.0 * np.cos(2.0 * np.pi * index / AZIM)).astype(np.float32)
    return table[order], np.ascontiguousarray(np.broadcast_to(mu[:, None], (AZIM, 128)))


def body(source, pressure_old, density, radial_forward, radial_back, radial_eig):
    table, mu = constants()
    anywhere = pl.BlockSpec(memory_space=pl.ANY)
    vmem = pl.BlockSpec(memory_space=pltpu.VMEM)
    dma = pltpu.SemaphoreType.DMA
    result = pl.pallas_call(
        kernel,
        out_shape=jax.ShapeDtypeStruct((ROWS * ROWS, AZIM), F32),
        in_specs=[anywhere] * 5 + [vmem] * 3,
        out_specs=anywhere,
        scratch_shapes=[
            pltpu.VMEM((AZIM, AZIM), BF16),
            pltpu.VMEM((AZIM, AZIM), BF16),
            pltpu.VMEM((ROWS, ROWS, AZIM), F32),
            pltpu.VMEM((ROWS + 2, ROWS, AZIM), F32),
            pltpu.VMEM((ROWS + 2, ROWS, AZIM), F32),
            pltpu.VMEM((2, 2, ROWS, AZIM), F32),
            pltpu.VMEM((2, 2, ROWS, AZIM), F32),
            pltpu.VMEM((UNIT, AZIM), BF16),
            pltpu.VMEM((UNIT, AZIM), BF16),
            pltpu.VMEM((CHUNKS, AZIM, UNIT), F32),
            pltpu.VMEM((2, CHUNKS, DEV, KW, UNIT), F32),
            pltpu.VMEM((ROWS * KW, MODES), BF16),
            pltpu.VMEM((ROWS * KW, MODES), BF16),
            pltpu.VMEM((2, ROWS, KW, MODES), F32),
            pltpu.VMEM((2, ROWS + 1, KW, MODES), F32),
            pltpu.VMEM((2, DEV, ROWS, MODES), F32),
            pltpu.VMEM((2, MODES, MODES), BF16),
            pltpu.VMEM((2, MODES, MODES), BF16),
            pltpu.VMEM((2 * ZC * KW, MODES), BF16),
            pltpu.VMEM((2, CHUNKS, MODES, ZC * KW), F32),
            pltpu.VMEM((2, CHUNKS, DEV, ROWS, ZC * KW), F32),
            pltpu.VMEM((ROWS * ROWS, AZIM), BF16),
            pltpu.VMEM((ROWS * ROWS, AZIM), BF16),
            pltpu.VMEM((ROWS * ROWS, AZIM), F32),
            pltpu.VMEM((2, 6, KW, MODES), F32),
            pltpu.VMEM((2, KW, MODES), F32),
            pltpu.VMEM((2, 2, KW, MODES), F32),
            pltpu.VMEM((2, 2, KW, LANES), F32),
            pltpu.VMEM((2, 8, 2, KW, LANES), F32),
            pltpu.VMEM((2, 8, KW, LANES), F32),
            pltpu.VMEM((2, 3, KW, LANES), F32),
            pltpu.VMEM((2, 3, KW, MODES), F32),
            dma((3,)), dma((2,)), dma((3, 2)), dma((3, 2)), dma((2,)), dma((2,)), dma((2, 4)),
            dma((2, 4)), dma((2, 4)), dma((2, 4)), dma((2, CHUNKS)), dma((2, CHUNKS)), dma((2, CHUNKS)),
            dma((2, CHUNKS)), dma((2, CHUNKS)), dma((2, CHUNKS)), dma((2,)), dma((2,)),
            dma((2,)), dma((2,)), dma((2,)), dma((2,)), dma((CHUNKS,)),
        ],
        compiler_params=pltpu.CompilerParams(
            collective_id=0, has_side_effects=True, vmem_limit_bytes=60 * 1024 * 1024
        ),
    )(
        source, pressure_old, density, radial_forward, radial_back,
        radial_eig, jnp.asarray(mu), jnp.asarray(table),
    )
    return result.reshape(ROWS, ROWS, AZIM)


def solution(mesh):
    in_specs = (
        P("axial", "radial", None),
        P("axial", "radial", None),
        P("axial", "radial", None),
        P("radial", None),
        P("radial", None),
        P(),
    )
    out_specs = P("axial", "radial", None)
    return jax.shard_map(body, mesh=mesh, in_specs=in_specs, out_specs=out_specs, check_vma=False)
```

```python
import functools

import jax
import jax.numpy as jnp
import numpy as np
from jax import lax
from jax.experimental import pallas as pl
from jax.experimental.pallas import tpu as pltpu
from jax.sharding import PartitionSpec as P

MESH = pl.DeviceIdType.MESH
F32, BF16 = jnp.float32, jnp.bfloat16
DEV = 16
ROWS = 48
AZIM = 256
MODES = 768
KW = 8
ZC = 16
CHUNKS = ROWS // ZC
TILES = 6
LANES = MODES // 2
UNIT = ZC * ROWS
OFFSETS = (
    (0, 1), (0, 3), (1, 0), (3, 0), (1, 1), (3, 3), (1, 3), (3, 1), (0, 2), (2, 0), (2, 2), (1, 2), (3, 2), (2, 1), (2, 3),
)
NT_DIMS = (((1,), (1,)), ((), ()))
NN_DIMS = (((1,), (0,)), ((), ()))


def split(x):
    hi = x.astype(BF16)
    return hi, (x - hi.astype(F32)).astype(BF16)


def dot3(ah, al, bh, bl, dims):
    def dot(a, b):
        return lax.dot_general(a, b, dims, preferred_element_type=F32)

    return dot(ah, bh) + (dot(ah, bl) + dot(al, bh))


def block_transpose(xs, width):
    lane = lax.broadcasted_iota(jnp.int32, xs[0].shape, 1)
    xs = list(xs)
    step = len(xs) // 2
    while step:
        shift = width * step
        low = (lane & shift) == 0
        for i in range(len(xs)):
            if i & step:
                continue
            a, b = xs[i], xs[i + step]
            if shift == 64:
                moved = pltpu.roll(jnp.where(low, b, a), 64, 1)
                xs[i], xs[i + step] = jnp.where(low, a, moved), jnp.where(low, moved, b)
            else:
                xs[i] = jnp.where(low, a, pltpu.roll(b, shift, 1))
                xs[i + step] = jnp.where(low, pltpu.roll(a, 128 - shift, 1), b)
        step //= 2
    return xs


def kernel(
    src_hbm, p_hbm, d_hbm, fwd_hbm, back_hbm, eig_ref, mu_ref, table_ref, out_hbm,
    th_ref, tl_ref, src, p, h, esend, ehalo, rh, rl, send, recv, xh, xl, spec, pw, mat, mh, ml, uu,
    bsend, brecv, yh, yl, out, cst, state, gsend, gpair, gchip, entry, csend, cin,
    load_sem, own_sem, halo_send, halo_recv, gat_send, gat_recv, z_send, z_recv, c_send, c_recv,
    f_send, f_recv, f_own, b_send, b_recv, b_own, x1_send, x1_recv, x2_send, x2_recv, x3_send, x3_recv, out_sem,
):
    ax, rad = lax.axis_index("axial"), lax.axis_index("radial")
    zz, core = ax // 2, ax % 2
    ry, rx = rad // 4, rad % 4

    def remote(src_ref, dst_ref, send_sem, recv_sem, device):
        return pltpu.make_async_remote_copy(
            src_ref=src_ref, dst_ref=dst_ref, send_sem=send_sem, recv_sem=recv_sem,
            device_id=device, device_id_type=MESH,
        )

    def await_bytes(ref, sem):
        pltpu.make_async_copy(ref, ref, sem).wait()

    def peers():
        for a, b in OFFSETS:
            yield ((ry + a + core * (b - a)) % 4) * 4 + (rx + b + core * (a - b)) % 4

    loads = [
        pltpu.make_async_copy(p_hbm, p.at[pl.ds(1, ROWS)], load_sem.at[0]),
        pltpu.make_async_copy(d_hbm, h.at[pl.ds(1, ROWS)], load_sem.at[1]),
        pltpu.make_async_copy(src_hbm, src, load_sem.at[2]),
    ]
    for load in loads:
        load.start()
    parity = (ry + rx) % 2
    slot = parity * 8 + ry * 2 + rx // 2
    chalf, shalf = zz % 4 % 2, zz % 4 // 2
    row_at = pl.multiple_of(24 * core, 8)
    col_at = pl.multiple_of(384 * chalf, 128)
    gives = (parity == shalf, parity != shalf)

    def own_piece(i):
        ref = (fwd_hbm, back_hbm)[i]
        return pltpu.make_async_copy(
            ref.at[pl.ds(row_at, 24), pl.ds(col_at, 384)],
            mat.at[i, slot, pl.ds(row_at, 24), pl.ds(col_at, 384)], own_sem.at[i],
        )

    for i in range(2):
        pl.when(gives[i])(lambda i=i: own_piece(i).start())

    barrier = pltpu.get_barrier_semaphore()

    def greet(o, carry):
        pl.semaphore_signal(barrier, inc=1, device_id=(ax, (rad + o) % DEV), device_id_type=MESH)
        pl.semaphore_signal(barrier, inc=1, device_id=((ax + o) % DEV, rad), device_id_type=MESH)
        return carry

    lax.fori_loop(1, DEV, greet, 0)

    loads[0].wait()
    loads[1].wait()

    def pack(z, carry):
        esend[0, 0, pl.ds(z, 1), :] = p[z + 1, ROWS - 1 : ROWS, :]
        esend[0, 1, pl.ds(z, 1), :] = 0.5 / h[z + 1, ROWS - 1 : ROWS, :]
        esend[1, 0, pl.ds(z, 1), :] = p[z + 1, 0:1, :]
        esend[1, 1, pl.ds(z, 1), :] = 0.5 / h[z + 1, 0:1, :]
        return carry

    lax.fori_loop(0, ROWS, pack, 0)

    pl.semaphore_wait(barrier, 2 * (DEV - 1))

    def z_halo(side, what):
        edge, slot, to = (ROWS - 1, 0, ax + 1) if side == 0 else (0, ROWS + 1, ax - 1)
        ref, dst = (p_hbm, p) if what == 0 else (d_hbm, h)
        return remote(
            ref.at[edge], dst.at[slot], halo_send.at[side, what], halo_recv.at[side, what], (to, rad)
        )

    def r_halo(side):
        to = rad + 1 if side == 0 else rad - 1
        return remote(
            esend.at[side], ehalo.at[side], halo_send.at[2, side], halo_recv.at[2, side], (ax, to)
        )

    has_above, has_below = ax < DEV - 1, ax > 0
    has_right, has_left = rad < DEV - 1, rad > 0

    @pl.when(has_right)
    def _():
        r_halo(0).start()

    @pl.when(has_left)
    def _():
        r_halo(1).start()

    @pl.when(has_above)
    def _():
        z_halo(0, 0).start()
        z_halo(0, 1).start()

    @pl.when(has_below)
    def _():
        z_halo(1, 0).start()
        z_halo(1, 1).start()

    def offer(i):
        @pl.when(gives[i])
        def _():
            own_piece(i).wait()
            piece = mat.at[i, slot, pl.ds(row_at, 24), pl.ds(col_at, 384)]
            for to in peers():
                remote(piece, piece, gat_send.at[i], gat_recv.at[i], (ax, to)).start()

    offer(0)
    offer(1)

    def weigh(z, carry):
        h[z + 1] = 0.5 / h[z + 1]
        return carry

    lax.fori_loop(0, ROWS, weigh, 0)
    for kh in range(2):
        mu = mu_ref[pl.ds(pl.multiple_of(rad * 2 * KW + kh * KW, 8), KW), :]
        half = 0.5 * (eig_ref[...].reshape(1, MODES) + jnp.concatenate([mu] * TILES, axis=1))
        grow = half + jnp.sqrt(half * (2.0 + half))
        theta = jnp.log1p(grow)
        cst[kh, 0] = theta
        cst[kh, 1] = grow / (1.0 + grow)
        pw[kh, 0] = jnp.ones((KW, MODES), F32)

        def power(j, kappa, kh=kh, theta=theta):
            now = jnp.exp(-(j.astype(F32) * theta))
            kappa = kappa + now * pw[kh, j - 1]
            pw[kh, j] = now
            return kappa

        cst[kh, 2] = lax.fori_loop(1, ROWS + 1, power, jnp.zeros((KW, MODES), F32))

    th_ref[...], tl_ref[...] = split(table_ref[...])
    loads[2].wait()

    @pl.when(has_below)
    def _():
        z_halo(0, 0).wait_recv()
        z_halo(0, 1).wait_recv()
        h[0] = 0.5 / h[0]

    @pl.when(jnp.logical_not(has_below))
    def _():
        p[0] = jnp.zeros((ROWS, AZIM), F32)
        h[0] = jnp.zeros((ROWS, AZIM), F32)

    @pl.when(has_above)
    def _():
        z_halo(1, 0).wait_recv()
        z_halo(1, 1).wait_recv()
        h[ROWS + 1] = 0.5 / h[ROWS + 1]

    @pl.when(jnp.logical_not(has_above))
    def _():
        p[ROWS + 1] = jnp.zeros((ROWS, AZIM), F32)
        h[ROWS + 1] = jnp.zeros((ROWS, AZIM), F32)

    @pl.when(has_left)
    def _():
        r_halo(0).wait_recv()

    @pl.when(jnp.logical_not(has_left))
    def _():
        ehalo[0] = jnp.zeros((2, ROWS, AZIM), F32)

    @pl.when(has_right)
    def _():
        r_halo(1).wait_recv()

    @pl.when(jnp.logical_not(has_right))
    def _():
        ehalo[1] = jnp.zeros((2, ROWS, AZIM), F32)

    def chip(step):
        return ((zz + step) % 8) * 2 + core

    def region(i, step, first, count):
        z4 = (zz + step) % 4
        return mat.at[
            i, pl.ds((z4 // 2 + i) % 2 * 8 + first, count), pl.ds(row_at, 24),
            pl.ds(pl.multiple_of(384 * (z4 % 2), 128), 384),
        ]

    def along(i, n):
        up, of, first, count = ((1, 0, 0, 8), (7, 0, 0, 8), (1, 7, 0, 4), (7, 1, 4, 4))[n]
        part = region(i, of, first, count)
        return remote(part, part, z_send.at[i, n], z_recv.at[i, n], (chip(up), rad))

    def swap(i, n):
        part = region(i, (0, 7, 1, 2)[n], 0, 8)
        return remote(part, part, c_send.at[i, n], c_recv.at[i, n], (zz * 2 + 1 - core, rad))

    def pass_on(i):
        @pl.when(gives[i])
        def _():
            await_bytes(mat.at[i, pl.ds(0, 7), pl.ds(0, 24), pl.ds(0, 384)], gat_recv.at[i])

        @pl.when(jnp.logical_not(gives[i]))
        def _():
            await_bytes(mat.at[i, pl.ds(0, 8), pl.ds(0, 24), pl.ds(0, 384)], gat_recv.at[i])

        for n in range(2):
            along(i, n).start()
        swap(i, 0).start()

    def pass_further(i):
        for n in range(2):
            await_bytes(region(i, 0, 0, 8), z_recv.at[i, n])
            along(i, 2 + n).start()
            swap(i, 1 + n).start()

    def pass_last(i):
        for n in range(2, 4):
            await_bytes(region(i, 0, 0, 4), z_recv.at[i, n])
        swap(i, 3).start()

    def split_mat(i):
        for n in range(4):
            await_bytes(region(i, 0, 0, 8), c_recv.at[i, n])

        def one(t, carry):
            y = t % 8 // 2
            x = t % 2 * 2 + (t // 8 + y) % 2
            at = pl.ds(pl.multiple_of((y * 4 + x) * ROWS, 16), ROWS)
            mh[i, at, :], ml[i, at, :] = split(mat[i, t])
            return carry

        lax.fori_loop(0, DEV, one, 0)

    row = lax.broadcasted_iota(jnp.int32, (ROWS, AZIM), 0)

    def ship_in(kh, c):
        for to in peers():
            remote(
                send.at[c, pl.ds(pl.multiple_of(kh * 128 + to * KW, 8), KW)], recv.at[kh, c, rad],
                f_send.at[kh, c], f_recv.at[kh, c], (ax, to),
            ).start()
        pltpu.make_async_copy(
            send.at[c, pl.ds(pl.multiple_of(kh * 128 + rad * KW, 8), KW)], recv.at[kh, c, rad],
            f_own.at[kh, c],
        ).start()

    def front(c, carry):
        def plane(z):
            mid_p, mid_h = p[z + 1], h[z + 1]
            base = 1.0 - mid_h

            def term(other_p, other_h):
                return (base - other_h) * (other_p - mid_p)

            def radial(side):
                edge = 0 if side == 0 else ROWS - 1
                shift = 1 if side == 0 else ROWS - 1
                return [
                    jnp.where(row == edge, ehalo[side, i, pl.ds(z, 1), :], pltpu.roll(mid, shift, 0))
                    for i, mid in enumerate((mid_p, mid_h))
                ]

            total = src[z] + term(p[z + 2], h[z + 2]) + term(p[z], h[z])
            total = total + term(*radial(1)) + term(*radial(0))
            total = total + term(pltpu.roll(mid_p, 1, 1), pltpu.roll(mid_h, 1, 1))
            return total + term(pltpu.roll(mid_p, AZIM - 1, 1), pltpu.roll(mid_h, AZIM - 1, 1))

        def cells(k, carry):
            parts = [split(plane(c * ZC + 2 * k + q)) for q in range(2)]
            for q, (hi, lo) in enumerate(parts):
                zl = 2 * k + q
                for j in range(3):
                    at = pl.multiple_of((zl // 8) * 384 + j * 128 + (zl % 8) * 16, 16)
                    rh[pl.ds(at, 16), :] = hi[16 * j : 16 * j + 16]
                    rl[pl.ds(at, 16), :] = lo[16 * j : 16 * j + 16]
            return carry

        lax.fori_loop(0, ZC // 2, cells, 0)
        for n in range(3):
            cols = pl.ds(256 * n, 256)
            send[c, :, cols] = dot3(th_ref[...], tl_ref[...], rh[cols, :], rl[cols, :], NT_DIMS)
        ship_in(0, c)

        for i in range(2):
            pl.when(c == 0)(functools.partial(pass_on, i))
        return carry

    lax.fori_loop(0, CHUNKS, front, 0)

    def second_half(c, carry):
        ship_in(1, c)
        return carry

    lax.fori_loop(0, CHUNKS, second_half, 0)
    pass_further(0)

    def regroup_in(kh, c):
        await_bytes(recv.at[0, 0, pl.ds(0, DEV - 1)], f_recv.at[kh, c])
        await_bytes(recv.at[0, 0, 0], f_own.at[kh, c])

        def one(hz, carry):
            groups = []
            for v in range(TILES):
                xs = []
                for e in range(8):
                    s, j = divmod(8 * v + e, 3)
                    xs.append(recv[kh, c, s, :, pl.ds(pl.multiple_of(hz * 384 + j * 128, 128), 128)])
                groups.append(xs)
            groups = [block_transpose(xs, 16) for xs in groups]
            for v, ys in enumerate(groups):
                for i in range(4):
                    at = pl.ds(pl.multiple_of(c * 128 + hz * 64 + i * 16, 16), 16)
                    y = jnp.concatenate(ys[2 * i : 2 * i + 2], axis=0)
                    xh[at, 128 * v : 128 * v + 128], xl[at, 128 * v : 128 * v + 128] = split(y)
            return carry

        lax.fori_loop(0, 2, one, 0)

    def half_lanes(which):
        return pl.ds(pl.multiple_of(which * LANES, 128), LANES)

    beside = (zz * 2 + 1 - core, rad)

    def to_beside(kh):
        return remote(
            gsend.at[kh, :, :, half_lanes(1 - core)], gpair.at[kh], x1_send.at[kh], x1_recv.at[kh], beside
        )

    def to_chips(kh, step):
        own = gchip.at[kh, zz]
        return remote(own, own, x2_send.at[kh], x2_recv.at[kh], (chip(step), rad))

    def answer(kh):
        return remote(
            csend.at[kh], cin.at[kh, :, :, half_lanes(core)], x3_send.at[kh], x3_recv.at[kh], beside
        )

    def both_blocks(kh):
        mine = [gsend[kh, i, :, half_lanes(core)] for i in range(2)]
        theirs = [gpair[kh, i] for i in range(2)]
        low = [jnp.where(core == 0, a, b) for a, b in zip(mine, theirs)]
        high = [jnp.where(core == 0, b, a) for a, b in zip(mine, theirs)]
        span, kappa = pw[kh, ROWS, :, half_lanes(core)], cst[kh, 2, :, half_lanes(core)]
        return low, high, span, kappa

    def join(kh):
        to_beside(kh).wait_recv()
        (low_g, low_u), (high_g, high_u), span, kappa = both_blocks(kh)
        gchip[kh, zz, 0] = high_g + span * low_g
        gchip[kh, zz, 1] = low_u + span * (high_u + kappa * low_g)

        def one(step, carry):
            to_chips(kh, step).start()
            return carry

        lax.fori_loop(1, 8, one, 0)

    def resolve(kh):
        await_bytes(gchip.at[kh, pl.ds(0, 7)], x2_recv.at[kh])
        (low_g, low_u), (high_g, high_u), span, kappa = both_blocks(kh)
        wide, kappa2 = span * span, kappa * (1.0 + span * span)
        enter = jnp.zeros((KW, LANES), F32)
        for z in range(8):
            entry[0, z] = enter
            enter = gchip[kh, z, 0] + wide * enter
        enter = jnp.zeros((KW, LANES), F32)
        for z in range(7, -1, -1):
            entry[1, z] = enter
            enter = gchip[kh, z, 1] + kappa2 * entry[0, z] + wide * enter
        th = cst[kh, 0, :, half_lanes(core)]
        ghost = enter * jnp.exp(-th) / (1.0 - jnp.exp(-float(2 * MODES + 2) * th))
        low_in, high_up = entry[0, zz], entry[1, zz]
        high_in = low_g + span * low_in
        low_up = high_u + kappa * high_in + span * high_up
        for i, (a, b) in enumerate(((low_in, high_in), (low_up, high_up), (ghost, ghost))):
            cin[kh, i, :, half_lanes(core)] = jnp.where(core == 0, a, b)
            csend[kh, i] = jnp.where(core == 0, b, a)
        answer(kh).start()

    def upward(kh, c, count):
        cells = pl.ds(c * ZC, count * ZC)
        part_rows = pl.ds(c * ZC * KW, count * ZC * KW)

        def transform(n, carry):
            rows = pl.ds(pl.multiple_of(256 * n, 256), 256)
            part = dot3(xh[part_rows, :], xl[part_rows, :], mh[0, rows, :], ml[0, rows, :], NT_DIMS)
            spec[kh, cells, :, rows] = part.reshape(count * ZC, KW, 256)
            return carry

        lax.fori_loop(0, 3, transform, 0)

        def sweep(z, carry):
            g, first = carry
            g = spec[kh, z] + g
            g = g - cst[kh, 1] * g
            spec[kh, z] = g
            return g, first + pw[kh, z] * g

        zero = jnp.zeros((KW, MODES), F32)
        begin = (zero, zero) if c == 0 else (gsend[kh, 0], gsend[kh, 1])
        last, first = lax.fori_loop(c * ZC, (c + count) * ZC, sweep, begin)
        gsend[kh, 0] = last
        gsend[kh, 1] = first

    def exchange(kh):
        to_beside(kh).start()
        join(kh)

    def enter(kh):
        answer(kh).wait_recv()
        below, above, ghost = cin[kh, 0], cin[kh, 1], cin[kh, 2]
        start = (ax * ROWS).astype(F32)
        cst[kh, 3] = below
        cst[kh, 4] = ghost * jnp.exp(-start * cst[kh, 0])
        cst[kh, 5] = ghost * jnp.exp(-(float(2 * MODES + 1 - ROWS) - start) * cst[kh, 0])

        state[kh] = above

    def lower(kh, c):
        def sweep(k, u):
            pair = ZC // 2 - 1 - k
            res = [None, None]
            for q in (1, 0):
                z = c * ZC + 2 * pair + q
                up, down = pw[kh, z + 1], pw[kh, ROWS - z]
                u = (spec[kh, z] + up * cst[kh, 3]) + (u - cst[kh, 1] * u)
                res[q] = u - cst[kh, 4] * up + cst[kh, 5] * down
            hi, lo = split(jnp.concatenate(res, axis=0))
            at = pl.multiple_of(pair * 2 * KW, 16)
            uu[pl.ds(at, 2 * KW), :] = hi
            uu[pl.ds(ZC * KW + at, 2 * KW), :] = lo
            return u

        state[kh] = lax.fori_loop(0, ZC // 2, sweep, state[kh])

        def transform(n, carry):
            rows = pl.ds(pl.multiple_of(256 * n, 256), 256)
            both = lax.dot_general(mh[1, rows, :], uu[...], NT_DIMS, preferred_element_type=F32)
            low = lax.dot_general(
                ml[1, rows, :], uu[: ZC * KW, :], NT_DIMS, preferred_element_type=F32
            )
            bsend[kh, c, rows, :] = both[:, : ZC * KW] + (both[:, ZC * KW :] + low)
            return carry

        lax.fori_loop(0, 3, transform, 0)
        for to in peers():
            remote(
                bsend.at[kh, c, pl.ds(pl.multiple_of(to * ROWS, 8), ROWS)], brecv.at[kh, c, rad],
                b_send.at[kh, c], b_recv.at[kh, c], (ax, to),
            ).start()
        pltpu.make_async_copy(
            bsend.at[kh, c, pl.ds(pl.multiple_of(rad * ROWS, 8), ROWS)], brecv.at[kh, c, rad],
            b_own.at[kh, c],
        ).start()

    def lower_rest(kh, count):
        def one(i, carry):
            lower(kh, count - 1 - i)
            return carry

        lax.fori_loop(0, count, one, 0)

    regroup_in(0, 0)
    regroup_in(0, 1)
    pass_last(0)
    pass_further(1)
    regroup_in(0, 2)
    split_mat(0)
    upward(0, 0, CHUNKS)
    exchange(0)
    pass_last(1)
    regroup_in(1, 0)
    regroup_in(1, 1)
    upward(1, 0, 2)
    resolve(0)
    split_mat(1)
    enter(0)
    lower(0, CHUNKS - 1)
    regroup_in(1, 2)
    upward(1, 2, 1)
    exchange(1)
    lower_rest(0, CHUNKS - 1)
    resolve(1)
    enter(1)
    lower_rest(1, CHUNKS)

    def regroup_out(kh, c):
        await_bytes(brecv.at[0, 0, pl.ds(0, DEV - 1)], b_recv.at[kh, c])
        await_bytes(brecv.at[0, 0, 0], b_own.at[kh, c])

        def one(rt, carry):
            xs = [brecv[kh, c, d, pl.ds(pl.multiple_of(rt * 16, 8), 16), :] for d in range(DEV)]
            for zl, y in enumerate(block_transpose(xs, 8)):
                at = pl.ds(pl.multiple_of(c * UNIT + zl * ROWS + rt * 16, 16), 16)
                yh[at, 128 * kh : 128 * kh + 128], yl[at, 128 * kh : 128 * kh + 128] = split(y)
            return carry

        lax.fori_loop(0, 3, one, 0)

    def early(i, carry):
        regroup_out(0, CHUNKS - 1 - i)
        return carry

    lax.fori_loop(0, CHUNKS, early, 0)

    def finish(i, carry):
        c = CHUNKS - 1 - i
        regroup_out(1, c)

        def transform(n, carry):
            rows = pl.ds(pl.multiple_of(c * UNIT + 256 * n, 256), 256)
            part = dot3(yh[rows, :], yl[rows, :], th_ref[...], tl_ref[...], NN_DIMS)
            out[rows, :] = part * (1.0 / AZIM)
            return carry

        lax.fori_loop(0, 3, transform, 0)
        at = pl.ds(pl.multiple_of(c * UNIT, 256), UNIT)
        pltpu.make_async_copy(out.at[at], out_hbm.at[at], out_sem.at[c]).start()
        return carry

    lax.fori_loop(0, CHUNKS, finish, 0)

    @pl.when(has_above)
    def _():
        z_halo(0, 0).wait_send()
        z_halo(0, 1).wait_send()

    @pl.when(has_below)
    def _():
        z_halo(1, 0).wait_send()
        z_halo(1, 1).wait_send()

    @pl.when(has_right)
    def _():
        r_halo(0).wait_send()

    @pl.when(has_left)
    def _():
        r_halo(1).wait_send()

    for i in range(2):

        @pl.when(gives[i])
        def _(i=i):
            await_bytes(mat.at[i, pl.ds(0, DEV - 1), pl.ds(0, 24), pl.ds(0, 384)], gat_send.at[i])

    for i in range(2):
        for n in range(4):
            along(i, n).wait_send()
            swap(i, n).wait_send()
    for kh in range(2):
        to_beside(kh).wait_send()
        await_bytes(gchip.at[kh, pl.ds(0, 7)], x2_send.at[kh])
        answer(kh).wait_send()

    def drain(c, carry):
        for kh in range(2):
            await_bytes(recv.at[0, 0, pl.ds(0, DEV - 1)], f_send.at[kh, c])
            await_bytes(brecv.at[0, 0, pl.ds(0, DEV - 1)], b_send.at[kh, c])
        at = pl.ds(pl.multiple_of(c * UNIT, 256), UNIT)
        pltpu.make_async_copy(out.at[at], out_hbm.at[at], out_sem.at[c]).wait()
        return carry

    lax.fori_loop(0, CHUNKS, drain, 0)


def constants():
    index = np.arange(AZIM)
    angle = 2.0 * np.pi * (index[:, None] * index[None, :] % AZIM) / AZIM
    table = (np.cos(angle) + np.sin(angle)).astype(np.float32)
    order = np.arange(AZIM).reshape(DEV, 2, KW).transpose(1, 0, 2).reshape(-1)
    mu = (2.0 - 2.0 * np.cos(2.0 * np.pi * index / AZIM)).astype(np.float32)
    return table[order], np.ascontiguousarray(np.broadcast_to(mu[:, None], (AZIM, 128)))


def body(source, pressure_old, density, radial_forward, radial_back, radial_eig):
    table, mu = constants()
    anywhere = pl.BlockSpec(memory_space=pl.ANY)
    vmem = pl.BlockSpec(memory_space=pltpu.VMEM)
    dma = pltpu.SemaphoreType.DMA
    result = pl.pallas_call(
        kernel,
        out_shape=jax.ShapeDtypeStruct((ROWS * ROWS, AZIM), F32),
        in_specs=[anywhere] * 5 + [vmem] * 3,
        out_specs=anywhere,
        scratch_shapes=[
            pltpu.VMEM((AZIM, AZIM), BF16),
            pltpu.VMEM((AZIM, AZIM), BF16),
            pltpu.VMEM((ROWS, ROWS, AZIM), F32),
            pltpu.VMEM((ROWS + 2, ROWS, AZIM), F32),
            pltpu.VMEM((ROWS + 2, ROWS, AZIM), F32),
            pltpu.VMEM((2, 2, ROWS, AZIM), F32),
            pltpu.VMEM((2, 2, ROWS, AZIM), F32),
            pltpu.VMEM((UNIT, AZIM), BF16),
            pltpu.VMEM((UNIT, AZIM), BF16),
            pltpu.VMEM((CHUNKS, AZIM, UNIT), F32),
            pltpu.VMEM((2, CHUNKS, DEV, KW, UNIT), F32),
            pltpu.VMEM((ROWS * KW, MODES), BF16),
            pltpu.VMEM((ROWS * KW, MODES), BF16),
            pltpu.VMEM((2, ROWS, KW, MODES), F32),
            pltpu.VMEM((2, ROWS + 1, KW, MODES), F32),
            pltpu.VMEM((2, DEV, ROWS, MODES), F32),
            pltpu.VMEM((2, MODES, MODES), BF16),
            pltpu.VMEM((2, MODES, MODES), BF16),
            pltpu.VMEM((2 * ZC * KW, MODES), BF16),
            pltpu.VMEM((2, CHUNKS, MODES, ZC * KW), F32),
            pltpu.VMEM((2, CHUNKS, DEV, ROWS, ZC * KW), F32),
            pltpu.VMEM((ROWS * ROWS, AZIM), BF16),
            pltpu.VMEM((ROWS * ROWS, AZIM), BF16),
            pltpu.VMEM((ROWS * ROWS, AZIM), F32),
            pltpu.VMEM((2, 6, KW, MODES), F32),
            pltpu.VMEM((2, KW, MODES), F32),
            pltpu.VMEM((2, 2, KW, MODES), F32),
            pltpu.VMEM((2, 2, KW, LANES), F32),
            pltpu.VMEM((2, 8, 2, KW, LANES), F32),
            pltpu.VMEM((2, 8, KW, LANES), F32),
            pltpu.VMEM((2, 3, KW, LANES), F32),
            pltpu.VMEM((2, 3, KW, MODES), F32),
            dma((3,)), dma((2,)), dma((3, 2)), dma((3, 2)), dma((2,)), dma((2,)), dma((2, 4)),
            dma((2, 4)), dma((2, 4)), dma((2, 4)), dma((2, CHUNKS)), dma((2, CHUNKS)), dma((2, CHUNKS)),
            dma((2, CHUNKS)), dma((2, CHUNKS)), dma((2, CHUNKS)), dma((2,)), dma((2,)),
            dma((2,)), dma((2,)), dma((2,)), dma((2,)), dma((CHUNKS,)),
        ],
        compiler_params=pltpu.CompilerParams(
            collective_id=0, has_side_effects=True, vmem_limit_bytes=60 * 1024 * 1024
        ),
    )(
        source, pressure_old, density, radial_forward, radial_back,
        radial_eig, jnp.asarray(mu), jnp.asarray(table),
    )
    return result.reshape(ROWS, ROWS, AZIM)


def solution(mesh):
    in_specs = (
        P("axial", "radial", None),
        P("axial", "radial", None),
        P("axial", "radial", None),
        P("radial", None),
        P("radial", None),
        P(),
    )
    out_specs = P("axial", "radial", None)
    return jax.shard_map(body, mesh=mesh, in_specs=in_specs, out_specs=out_specs, check_vma=False)
```
